256 devices in a mesh: dp: 8 (over x, core), ctx: 32 (over y, z).
Axes of the slice: x: 4, y: 4, z: 8, core: 2. Of those that a mesh axis runs over, the one named last changes fastest.
Arguments:
- grad_out: bfloat16 [8, 10240, 2048], P('dp', 'ctx'), may hold values from -6 to 6
- chosen: int32 [8, 2560], P('dp', 'ctx'), may hold values from 0 to 319, as said below
- counts: int32 [8, 32], P('dp', 'ctx'), may hold values from 1 to 80, 1280 in all within a row
- queries: bfloat16 [8, 2560, 1024], P('dp', 'ctx'), may hold values from -136 to 136
- keys: bfloat16 [8, 2560, 1024], P('dp', 'ctx'), may hold values from -4 to 4
- values: bfloat16 [8, 2560, 1024], P('dp', 'ctx'), may hold values from -6 to 6
- router_logit: float32 [8, 2560], P('dp', 'ctx'), may hold values from -8 to 8
- out_weight: bfloat16 [1024, 2048], replicated, may hold values from -0.1875 to 0.1875
Outputs:
- d_queries: bfloat16 [8, 2560, 1024], P('dp', 'ctx')
- d_keys: bfloat16 [8, 2560, 1024], P('dp', 'ctx')
- d_values: bfloat16 [8, 2560, 1024], P('dp', 'ctx')
- d_logit: float32 [8, 2560], P('dp', 'ctx')
- d_weight: float32 [1024, 2048], P(None, 'ctx')
The draws below stay inside these ranges and needn't reach their ends.
Inputs may be any that keep to these rules, and one draw needn't show every extreme that they name: Each ctx shard's 80 entries are distinct local positions in ascending order; the first counts of them are that shard's chosen tokens. The counts of one sequence sum to 1280.
All inputs are finite; a program needn't handle non-finite values. No bound on the sum of `counts` on one device may be relied on, other than what follows from the above.
Results may differ from the reference program's by a relative error of at most 0.03.
Values may be sent and summed in bfloat16 or wider, within the bound.
A program may use at most 192 MiB of HBM per device.

```python
import math
import jax
import jax.numpy as jnp
import numpy as np
from jax import lax

D = 2048
HEADS = 8
HEAD_DIM = 128
TOK_DEV = 320
CAP = 80
CHOSEN = 1280
SLOTS = 2560
TOKENS = 10240
SEQS = 8
QKV_WIDTH = 1024
N_CTX = 32


def shared_bases(key):
    base_query = jnp.clip(jax.random.normal(jax.random.fold_in(key, 11), (SEQS, SLOTS, QKV_WIDTH), jnp.float32), -4.0, 4.0)
    base_key = jnp.clip(jax.random.normal(jax.random.fold_in(key, 12), (SEQS, SLOTS, QKV_WIDTH), jnp.float32), -4.0, 4.0)
    return (base_query, base_key)


def draw_queries(key, part):
    base_query, base_key = shared_bases(key)
    result = base_query
    return result.astype(jnp.bfloat16)


def draw_keys(key, part):
    base_query, base_key = shared_bases(key)
    result = base_key
    return result.astype(jnp.bfloat16)


def draw_chosen(key, part):
    key = jax.random.fold_in(key, 5)
    shard_keys = jax.random.split(key, SEQS * (SLOTS // CAP))
    orders = jax.vmap(lambda single: jax.random.permutation(single, TOK_DEV))(shard_keys)
    picked = jnp.sort(orders[:, :CAP], axis=1)
    return picked.reshape(SEQS, SLOTS).astype(jnp.int32)


def shard_levels(key, extent, pieces, smallest, largest):
    gain = 1.0
    for axis_at, shards_of in pieces:
        heights = jax.random.uniform(jax.random.fold_in(jax.random.fold_in(key, 6), axis_at), (shards_of,), jnp.float32, smallest / len(pieces), largest / len(pieces))
        gain = gain * jnp.repeat(jnp.exp(heights), extent[axis_at] // shards_of).reshape((-1,) + (1,) * (len(extent) - 1 - axis_at))
    return gain


def profile(amount, total, most, skew):
    weights = [(1 << 20) // math.isqrt(rank ** skew) + 1 for rank in range(2, amount + 1)]
    spare, holding = total - most - (amount - 1), [1] * (amount - 1)
    while spare > 0:
        free = [i for i in range(amount - 1) if holding[i] < most]
        pool, budget = sum([weights[i] for i in free]), spare
        for i in free:
            extra = min(most - holding[i], max(1, budget * weights[i] // pool), spare)
            holding[i] = holding[i] + extra
            spare = spare - extra
    return np.array([most] + holding)


def uneven(key, count, total, bound, slope):
    if count == 2:
        one = jax.random.randint(key, (), max(1, total - bound), min(bound, total - 1) + 1)
        return jnp.stack([one, total - one])
    sizes = jnp.asarray(profile(count, total, bound, slope), jnp.int32)
    twos = (count - 1) // 2
    donor, receiver = sizes[1:1 + 2 * twos:2], sizes[2:2 + 2 * twos:2]
    slack = jnp.minimum(donor - 1, bound - receiver)
    passed = jax.random.randint(jax.random.fold_in(key, 1), (twos,), 0, 1 << 20) % (slack + 1)
    sizes = sizes.at[1:1 + 2 * twos:2].set(donor - passed).at[2:2 + 2 * twos:2].set(receiver + passed)
    return sizes[jax.random.permutation(jax.random.fold_in(key, 2), count)]


def normal_values(own_key, shape, deviation, reach, pieces=(), kind=jnp.bfloat16):
    drawn = jax.random.normal(own_key, shape, jnp.float32) * deviation
    if len(pieces) > 0:
        drawn = shard_levels(own_key, shape, pieces, -0.22, 0.18) * drawn
    return jnp.clip(drawn, min=-reach, max=reach).astype(kind)


def setup_inputs(seed: int = 0) -> dict:
    arg_keys = jax.random.split(jax.random.key(seed), 9)
    grad_out = normal_values(arg_keys[0], (SEQS, TOKENS, D), 1.0, 6.0, ((0, 8), (1, 32)))
    chosen = draw_chosen(jax.random.fold_in(arg_keys[8], 71), 0)
    counts = jax.vmap(lambda own: uneven(own, N_CTX, CHOSEN, CAP, 2))(jax.random.split(arg_keys[2], SEQS)).reshape((SEQS, N_CTX)).astype(jnp.int32)
    queries = draw_queries(jax.random.fold_in(arg_keys[8], 71), 0)
    keys = draw_keys(jax.random.fold_in(arg_keys[8], 71), 0)
    values = normal_values(arg_keys[5], (SEQS, SLOTS, QKV_WIDTH), 1.0, 6.0, ((0, 8), (1, 32)))
    router_logit = normal_values(arg_keys[6], (SEQS, SLOTS), 2.0, 8.0, ((0, 8), (1, 32)), jnp.float32)
    out_weight = normal_values(arg_keys[7], (QKV_WIDTH, D), QKV_WIDTH ** -0.5, 0.1875)
    return {"grad_out": grad_out, "chosen": chosen, "counts": counts, "queries": queries, "keys": keys, "values": values, "router_logit": router_logit, "out_weight": out_weight}


NEG_FILL = -1.0e30


def one_sequence(items):
    grad_rows, chosen_row, count_row, query_rows, key_rows, value_rows, logit_row, out_weight = items
    scale = 1.0 / (HEAD_DIM ** 0.5)
    slot_ids = jnp.arange(SLOTS, dtype=jnp.int32)
    shard_ids = slot_ids // CAP
    live = (slot_ids % CAP) < count_row[shard_ids]
    positions = (shard_ids * TOK_DEV + chosen_row).astype(jnp.int32)
    picked = jnp.where(live[:, None], grad_rows[positions], jnp.zeros((), grad_rows.dtype)).astype(jnp.bfloat16)
    query_heads = query_rows.astype(jnp.float32).reshape(SLOTS, HEADS, HEAD_DIM)
    key_heads = key_rows.astype(jnp.float32).reshape(SLOTS, HEADS, HEAD_DIM)
    value_heads = value_rows.astype(jnp.float32).reshape(SLOTS, HEADS, HEAD_DIM)
    allowed = (live[:, None] & live[None, :] & (slot_ids[None, :] <= slot_ids[:, None])) | (slot_ids[None, :] == slot_ids[:, None])
    scores = jnp.einsum('qhd,khd->hqk', query_heads, key_heads) * scale
    scores = jnp.where(allowed[None], scores, NEG_FILL)
    row_max = jnp.max(scores, axis=2, keepdims=True)
    expo = jnp.where(allowed[None], jnp.exp(scores - row_max), 0.0)
    probs = expo / jnp.sum(expo, axis=2, keepdims=True)
    probs_b = probs.astype(jnp.bfloat16)
    attended = jnp.einsum('hqk,khd->qhd', probs_b.astype(jnp.float32), value_heads).reshape(SLOTS, QKV_WIDTH).astype(jnp.bfloat16)
    projected = jnp.dot(attended, out_weight, preferred_element_type=jnp.float32)
    gate = jax.nn.sigmoid(logit_row)
    d_logit = jnp.where(live, gate * (1.0 - gate) * jnp.sum(picked.astype(jnp.float32) * projected, axis=1), 0.0)
    d_block = (gate[:, None] * picked.astype(jnp.float32)).astype(jnp.bfloat16)
    d_weight = jnp.dot(attended.T, d_block, preferred_element_type=jnp.float32)
    d_attended = jnp.dot(d_block, out_weight.T, preferred_element_type=jnp.float32).astype(jnp.bfloat16)
    d_att_heads = d_attended.astype(jnp.float32).reshape(SLOTS, HEADS, HEAD_DIM)
    delta = jnp.sum(d_att_heads * attended.astype(jnp.float32).reshape(SLOTS, HEADS, HEAD_DIM), axis=2)
    d_probs = jnp.einsum('qhd,khd->hqk', d_att_heads, value_heads)
    d_scores = (probs * (d_probs - delta.T[:, :, None]) * scale).astype(jnp.bfloat16).astype(jnp.float32)
    d_queries = jnp.einsum('hqk,khd->qhd', d_scores, key_heads).reshape(SLOTS, QKV_WIDTH).astype(jnp.bfloat16)
    d_keys = jnp.einsum('hqk,qhd->khd', d_scores, query_heads).reshape(SLOTS, QKV_WIDTH).astype(jnp.bfloat16)
    d_values = jnp.einsum('hqk,qhd->khd', probs_b.astype(jnp.float32), d_att_heads).reshape(SLOTS, QKV_WIDTH).astype(jnp.bfloat16)
    return d_queries, d_keys, d_values, d_logit, d_weight


def reference(grad_out, chosen, counts, queries, keys, values, router_logit, out_weight):
    weights = jnp.broadcast_to(out_weight[None], (SEQS,) + out_weight.shape)
    d_queries, d_keys, d_values, d_logit, d_weight = lax.map(one_sequence, (grad_out, chosen, counts, queries, keys, values, router_logit, weights))
    return d_queries, d_keys, d_values, d_logit, jnp.sum(d_weight, axis=0)
```

```python
import functools
import math

import jax
import jax.numpy as jnp
from jax import lax
from jax.experimental import pallas as pl
from jax.experimental.pallas import tpu as pltpu
from jax.sharding import PartitionSpec as P

MESH = pl.DeviceIdType.MESH
HD = 128
CORES = 2
NEG = -1e30
F32 = jnp.float32
BF16 = jnp.bfloat16


def rows_dot(a, b):
    return lax.dot_general(a, b, (((1,), (1,)), ((), ())), preferred_element_type=F32)


def dot(a, b):
    return jnp.dot(a, b, preferred_element_type=F32)


def turned(a):
    return jnp.transpose(a.astype(F32)).astype(a.dtype)


def kernel(
    dims,
    grad_hbm, chosen_ref, counts_ref, q_hbm, k_hbm, v_hbm, logit_ref, w_hbm,
    dq_hbm, dk_hbm, dv_hbm, dlogit_ref, dw_ref,
    grad_v, w_v, own_v, got_v, far_v, kb_v, kc_v, vc_v, qc_v, qb_v,
    d_all, da_send, da_v, s_v, p_v, m_v, a_v, dan_v, dl_send, dl_got, c_v, delta_v,
    ds_v, dq_acc, dq_send, part_send, part_got, own_dk, own_dv, dkv_send,
    a_all, t_send, t_got, t_own, z_send, z_got, w_all,
    load_sem, big_sem, send1, recv1, fsend, frecv, dasend, darecv, dsend, drecv,
    asend, arecv, lsend, lrecv, psend, precv, qsend, qrecv, kvsend, kvrecv,
    tsend, trecv, zsend, zrecv, wsend, wrecv,
):
    DP, Y, Z, CAP, PB = dims
    X = DP // CORES
    NQ = Z * CAP
    NB = Z // PB
    BR = PB * CAP
    dp = lax.axis_index("dp")
    ctx = lax.axis_index("ctx")
    y = lax.div(ctx, Z)
    z = lax.rem(ctx, Z)
    x = lax.div(dp, CORES)
    core = lax.rem(dp, CORES)
    width = Z * HD
    model = w_v.shape[1]
    cols_y = model // Y
    cols = cols_y // Z
    scale = 1.0 / math.sqrt(HD)
    c2 = scale * math.log2(math.e)

    def at(yy, zz):
        return yy * Z + zz

    def remote(src, dst, ss, rs, to_dp, to_ctx):
        return pltpu.make_async_remote_copy(
            src_ref=src, dst_ref=dst, send_sem=ss, recv_sem=rs,
            device_id=(to_dp, to_ctx), device_id_type=MESH,
        )

    def arrived(dst, rs):
        remote(dst, dst, rs, rs, dp, ctx).wait_recv()

    def left(src, ss):
        remote(src, src, ss, ss, dp, ctx).wait_send()

    def offset(i):
        half = lax.div(i + 1, 2)
        odd = lax.rem(i, 2)
        return odd * half + (1 - odd) * lax.rem(Z - half, Z)

    def head_cols(h):
        return pl.ds(pl.multiple_of(h * HD, HD), HD)

    barrier = pltpu.get_barrier_semaphore()

    def greet(to_dp, to_ctx):
        pl.semaphore_signal(barrier, inc=1, device_id=(to_dp, to_ctx), device_id_type=MESH)

    @pl.loop(1, Z)
    def _(i):
        greet(dp, at(y, lax.rem(z + i, Z)))

    @pl.loop(1, Y)
    def _(i):
        greet(dp, at(lax.rem(y + i, Y), z))

    @pl.loop(1, DP)
    def _(i):
        greet(lax.rem(dp + i, DP), ctx)

    @pl.loop(0, DP)
    def _(s):
        @pl.when(jnp.logical_not((s == dp) & (z == dp)))
        def _():
            greet(s, at(y, dp))

    @pl.loop(0, Z)
    def _(h):
        pltpu.make_async_copy(k_hbm.at[0, :, head_cols(h)], own_v.at[h, pl.ds(0, CAP)], load_sem.at[0, h]).start()
        pltpu.make_async_copy(v_hbm.at[0, :, head_cols(h)], own_v.at[h, pl.ds(CAP, CAP)], load_sem.at[1, h]).start()
        pltpu.make_async_copy(
            q_hbm.at[0, :, head_cols(h)], own_v.at[h, pl.ds(2 * CAP + 16, CAP)], load_sem.at[2, h]
        ).start()

    pltpu.make_async_copy(grad_hbm.at[0], grad_v, big_sem.at[0]).start()
    pltpu.make_async_copy(w_hbm, w_v, big_sem.at[1]).start()
    count = counts_ref[0, 0].astype(F32)

    @pl.loop(0, Z)
    def _(h):
        own_v[h, pl.ds(2 * CAP, 16), :] = jnp.full((16, HD), count, F32).astype(BF16)

    @pl.loop(0, Z)
    def _(h):
        for which, first in ((0, 0), (1, CAP), (2, 2 * CAP + 16)):
            pltpu.make_async_copy(
                q_hbm.at[0, :, head_cols(h)], own_v.at[h, pl.ds(first, CAP)], load_sem.at[which, h]
            ).wait()

    pl.semaphore_wait(barrier, (Z - 1) + (Y - 1) + (DP - 1) + DP - (dp == z).astype(jnp.int32))

    @pl.loop(1, Z)
    def _(i):
        to = lax.rem(z + offset(i), Z)
        remote(own_v.at[to], got_v.at[z], send1.at[to], recv1.at[z], dp, at(y, to)).start()

    pltpu.make_async_copy(own_v.at[z], got_v.at[z], recv1.at[z]).start()

    eye = lax.broadcasted_iota(jnp.int32, (CAP, CAP), 0) == lax.broadcasted_iota(jnp.int32, (CAP, CAP), 1)

    def column(row):
        return jnp.sum(jnp.where(eye, row, 0.0), axis=1, keepdims=True)

    gate_row = jax.nn.sigmoid(logit_ref[...])
    live_col = lax.broadcasted_iota(jnp.int32, (CAP, 1), 0).astype(F32) < count
    chosen_col = column(chosen_ref[...].astype(F32))
    toks = grad_v.shape[0]
    hot = jnp.where(
        (lax.broadcasted_iota(jnp.int32, (CAP, toks), 1).astype(F32) == chosen_col) & live_col, 1.0, 0.0
    ).astype(BF16)
    gate_col = column(gate_row)
    pltpu.make_async_copy(grad_hbm.at[0], grad_v, big_sem.at[0]).wait()
    half = model // 2

    @pl.loop(0, 2)
    def _(i):
        part = pl.ds(pl.multiple_of(i * half, HD), half)
        d_all[dp, :, part] = (gate_col * dot(hot, grad_v[:, part])).astype(BF16)

    @pl.loop(1, X)
    def _(i):
        to = lax.rem(x + i, X) * CORES + core
        remote(d_all.at[dp], d_all.at[dp], dsend.at[i], drecv.at[dp], to, ctx).start()

    other = x * CORES + (1 - core)
    remote(d_all.at[dp], d_all.at[dp], dsend.at[0], drecv.at[dp], other, ctx).start()

    lane = lax.broadcasted_iota(jnp.int32, (1, NQ), 1).astype(F32)

    def live_lanes(zz, cnt):
        base = (zz * CAP).astype(F32)
        return (lane >= base) & (lane - base < cnt)

    def later_y(i):
        return y + i < Y

    pltpu.make_async_copy(w_hbm, w_v, big_sem.at[1]).wait()

    def step(i, kb):
        off = offset(i)
        to = lax.rem(z + off, Z)
        frm = lax.rem(z + Z - off, Z)
        w_h = w_v[pl.ds(pl.multiple_of(to * HD, HD), HD), :]
        da = rows_dot(d_all[dp], w_h).astype(BF16)
        da_send[to] = da

        @pl.when(i > 0)
        def _():
            remote(da_send.at[to], da_v.at[z], dasend.at[to], darecv.at[z], dp, at(y, to)).start()

        @pl.when(i == 0)
        def _():
            da_v[z] = da

        arrived(got_v.at[frm], recv1.at[frm])

        @pl.loop(1, Y)
        def _(j):
            @pl.when(later_y(j))
            def _():
                kv = pl.ds(0, 2 * CAP + 16)
                remote(
                    got_v.at[frm, kv], far_v.at[j - 1, frm], fsend.at[j - 1, frm], frecv.at[j - 1, frm],
                    dp, at(y + j, z),
                ).start()

        kc_v[0, frm] = got_v[frm, pl.ds(0, CAP), :]
        vc_v[0, frm] = got_v[frm, pl.ds(CAP, CAP), :]
        qc_v[frm] = got_v[frm, pl.ds(2 * CAP + 16, CAP), :]
        cnt = got_v[frm, pl.ds(2 * CAP, 16), :].astype(F32)[0:1, 0:1]
        rows = lax.broadcasted_iota(jnp.int32, (CAP, 1), 0).astype(F32)
        qb_v[frm] = jnp.where(rows < cnt, 0.0, NEG)
        return jnp.where(live_lanes(frm, cnt), 0.0, kb)

    kb0 = lax.fori_loop(0, Z, step, jnp.full((1, NQ), NEG, F32))
    kb_v[0] = jnp.broadcast_to(kb0, (8, NQ))

    def flat(a):
        return a.reshape(a.shape[0] * a.shape[1], a.shape[2])

    def blocks(a):
        return a.reshape(PB, CAP, a.shape[1])

    @pl.loop(0, NB)
    def _(b):
        some = pl.ds(b * PB, PB)
        s = rows_dot(flat(qc_v[some]), flat(kc_v[0]))
        qb = flat(qb_v[some])
        row = lax.broadcasted_iota(jnp.int32, (BR, NQ), 0) + b * BR
        col = lax.broadcasted_iota(jnp.int32, (BR, NQ), 1)
        masked = jnp.where(col < row, s + kb_v[0, 0:1, :] + qb, NEG)
        s = jnp.where(col == row, s, masked)
        s_v[0, some] = blocks(s)
        m_v[some] = blocks(jnp.max(s, axis=1, keepdims=True))

    def earlier(d, _):
        @pl.loop(0, Z)
        def _(zz):
            arrived(far_v.at[d - 1, zz], frecv.at[d - 1, zz])

        def bring(zz, kb):
            kc_v[d, zz] = far_v[d - 1, zz, pl.ds(0, CAP), :]
            vc_v[d, zz] = far_v[d - 1, zz, pl.ds(CAP, CAP), :]
            cnt = far_v[d - 1, zz, pl.ds(2 * CAP, 16), :].astype(F32)[0:1, 0:1]
            return jnp.where(live_lanes(zz, cnt), 0.0, kb)

        kb = lax.fori_loop(0, Z, bring, jnp.full((1, NQ), NEG, F32))

        @pl.loop(0, NB)
        def _(b):
            some = pl.ds(b * PB, PB)
            s = rows_dot(flat(qc_v[some]), flat(kc_v[d])) + kb
            s_v[d, some] = blocks(s)
            top = jnp.max(s, axis=1, keepdims=True) + flat(qb_v[some])
            m_v[some] = blocks(jnp.maximum(flat(m_v[some]), top))

        return 0

    lax.fori_loop(1, y + 1, earlier, 0)

    @pl.loop(1, X)
    def _(i):
        frm = lax.rem(x + i, X) * CORES + core
        arrived(d_all.at[frm], drecv.at[frm])
        remote(d_all.at[frm], d_all.at[frm], dsend.at[X - 1 + i], drecv.at[frm], other, ctx).start()

    @pl.loop(1, Z)
    def _(i):
        frm = lax.rem(z + i, Z)
        arrived(da_v.at[frm], darecv.at[frm])

    wide = lax.broadcasted_iota(jnp.int32, (CAP, HD), 0) == lax.broadcasted_iota(jnp.int32, (CAP, HD), 1)

    @pl.loop(0, NB)
    def _(b):
        some = pl.ds(b * PB, PB)
        mc = flat(m_v[some]) * c2
        qb = flat(qb_v[some])

        def one(d, carry):
            total, o = carry
            top = mc - jnp.where(d > 0, qb, 0.0)
            p = jnp.exp2(flat(s_v[d, some]) * c2 - top)
            pb = p.astype(BF16)
            p_v[d, some] = blocks(pb)
            return total + jnp.sum(p, axis=1, keepdims=True), o + dot(pb, flat(vc_v[d]))

        total, o = lax.fori_loop(0, y + 1, one, (jnp.zeros((BR, 1), F32), jnp.zeros((BR, HD), F32)))
        inv = 1.0 / total
        att = (o * inv).astype(BF16)
        a_v[some] = blocks(att)
        da = flat(da_v[some]).astype(F32)
        delta = jnp.sum(da * att.astype(F32), axis=1, keepdims=True)
        delta_v[some] = blocks(delta)
        c_v[some] = blocks(inv * scale)
        dan_v[some] = blocks((da * inv).astype(BF16))
        for k in range(PB):
            mine = delta[k * CAP : (k + 1) * CAP]
            row = jnp.sum(jnp.where(wide, mine, 0.0), axis=0, keepdims=True)
            dl_send[b * PB + k] = jnp.broadcast_to(row, (8, HD))

    @pl.loop(0, Z)
    def _(i):
        to = lax.rem(z + i, Z)

        @pl.when(jnp.logical_not((dp == z) & (i == 0)))
        def _():
            remote(a_v.at[to], a_all.at[dp], asend.at[to], arecv.at[dp], z, at(y, to)).start()

        @pl.when(i > 0)
        def _():
            remote(dl_send.at[to], dl_got.at[z], lsend.at[to], lrecv.at[z], dp, at(y, to)).start()

    @pl.when(dp == z)
    def _():
        a_all[dp] = a_v[z]

    dl_got[z] = dl_send[z]

    q_t = turned(flat(qc_v[...]))
    da_t = turned(flat(dan_v[...]))
    dq_acc[...] = jnp.zeros_like(dq_acc)

    def backward(d):
        @pl.loop(0, NB)
        def _(b):
            some = pl.ds(b * PB, PB)
            dprobs = rows_dot(flat(da_v[some]), flat(vc_v[d]))
            ds = flat(p_v[d, some]).astype(F32) * ((dprobs - flat(delta_v[some])) * flat(c_v[some]))
            ds = ds.astype(BF16)
            ds_v[some] = blocks(ds)
            dq_acc[some] += blocks(dot(ds, flat(kc_v[d])))

        dk_t = dot(q_t, flat(ds_v[...]))
        dv_t = dot(da_t, flat(p_v[d]))
        return jnp.transpose(dk_t), jnp.transpose(dv_t)

    def pieces(a):
        return a.reshape(Z, CAP, HD)

    def far(i, _):
        d = y + 1 - i
        dk, dv = backward(d)
        part_send[d - 1, 0] = pieces(dk.astype(BF16))
        part_send[d - 1, 1] = pieces(dv.astype(BF16))
        remote(
            part_send.at[d - 1], part_got.at[d - 1], psend.at[d - 1], precv.at[d - 1], dp, at(y - d, z)
        ).start()
        return 0

    lax.fori_loop(1, y + 1, far, 0)

    @pl.loop(0, DP)
    def _(s):
        @pl.when(jnp.logical_not((s == dp) & (z == dp)))
        def _():
            arrived(a_all.at[s], arecv.at[s])

    @pl.loop(0, X)
    def _(i):
        frm = lax.rem(x + i, X) * CORES + 1 - core
        arrived(d_all.at[frm], drecv.at[frm])

    a_t = turned(flat(a_all[...]))

    @pl.loop(1, Y + 1)
    def _(i):
        to = lax.rem(y + i, Y)
        t = dot(a_t, flat(d_all[:, :, pl.ds(pl.multiple_of(to * cols_y, HD), cols_y)]))

        @pl.when(i < Y)
        def _():
            t_send[i - 1] = t.astype(BF16)
            remote(t_send.at[i - 1], t_got.at[i - 1], tsend.at[i - 1], trecv.at[i - 1], dp, at(to, z)).start()

        @pl.when(i == Y)
        def _():
            t_own[...] = t

    dk, dv = backward(0)
    own_dk[...] = pieces(dk)
    own_dv[...] = pieces(dv)
    dq_send[...] = dq_acc[...].astype(BF16)

    @pl.loop(0, Z)
    def _(i):
        to = lax.rem(z + i, Z)

        @pl.when(i > 0)
        def _():
            remote(dq_send.at[to], dq_hbm.at[0, :, head_cols(z)], qsend.at[to], qrecv.at[z], dp, at(y, to)).start()

        @pl.when(i == 0)
        def _():
            pltpu.make_async_copy(dq_send.at[z], dq_hbm.at[0, :, head_cols(z)], qrecv.at[z]).start()

    @pl.loop(0, Y - 1)
    def _(i):
        arrived(t_got.at[i], trecv.at[i])

    t_all = t_own[...]
    for i in range(Y - 1):
        t_all = t_all + t_got[i].astype(F32)
    z_send[...] = jnp.transpose(t_all).astype(BF16).reshape(Z, cols, HD)

    @pl.loop(1, Z)
    def _(i):
        to = lax.rem(z + i, Z)
        remote(z_send.at[to], z_got.at[z], zsend.at[to], zrecv.at[z], dp, at(y, to)).start()

    z_got[z] = z_send[z]

    def add(d, _):
        arrived(part_got.at[d - 1], precv.at[d - 1])
        own_dk[...] += part_got[d - 1, 0].astype(F32)
        own_dv[...] += part_got[d - 1, 1].astype(F32)
        return 0

    lax.fori_loop(1, Y - y, add, 0)
    dkv_send[0] = own_dk[...].astype(BF16)
    dkv_send[1] = own_dv[...].astype(BF16)

    @pl.loop(0, Z)
    def _(i):
        to = lax.rem(z + i, Z)
        for which, out in ((0, dk_hbm), (1, dv_hbm)):

            @pl.when(i > 0)
            def _():
                remote(
                    dkv_send.at[which, to], out.at[0, :, head_cols(z)], kvsend.at[which, to], kvrecv.at[which, z],
                    dp, at(y, to),
                ).start()

            @pl.when(i == 0)
            def _():
                pltpu.make_async_copy(
                    dkv_send.at[which, z], out.at[0, :, head_cols(z)], kvrecv.at[which, z]
                ).start()

    @pl.loop(1, Z)
    def _(i):
        frm = lax.rem(z + i, Z)
        arrived(z_got.at[frm], zrecv.at[frm])

    tile = z_got[0].astype(F32)
    for i in range(1, Z):
        tile = tile + z_got[i].astype(F32)
    w_all[dp] = tile

    @pl.loop(1, DP)
    def _(i):
        to = lax.rem(dp + i, DP)
        remote(w_all.at[dp], w_all.at[dp], wsend.at[i], wrecv.at[dp], to, ctx).start()

    @pl.loop(1, Z)
    def _(i):
        frm = lax.rem(z + i, Z)
        arrived(dl_got.at[frm], lrecv.at[frm])

    delta_sum = dl_got[0]
    for i in range(1, Z):
        delta_sum = delta_sum + dl_got[i]
    live_row = lax.broadcasted_iota(jnp.int32, (1, CAP), 1).astype(F32) < count
    dlogit_ref[...] = jnp.where(live_row, (1.0 - gate_row) * delta_sum[0:1, 0:CAP], 0.0)

    @pl.loop(1, DP)
    def _(i):
        frm = lax.rem(dp + i, DP)
        arrived(w_all.at[frm], wrecv.at[frm])

    for h in range(DP):
        dw_ref[pl.ds(h * HD, HD), :] = jnp.transpose(w_all[h])

    @pl.loop(0, Z)
    def _(i):
        arrived(dq_hbm.at[0, :, head_cols(i)], qrecv.at[i])
        arrived(dk_hbm.at[0, :, head_cols(i)], kvrecv.at[0, i])
        arrived(dv_hbm.at[0, :, head_cols(i)], kvrecv.at[1, i])

    @pl.loop(1, Z)
    def _(i):
        to = lax.rem(z + i, Z)
        left(own_v.at[to], send1.at[to])
        left(da_send.at[to], dasend.at[to])
        left(dl_send.at[to], lsend.at[to])
        left(dq_send.at[to], qsend.at[to])
        left(z_send.at[to], zsend.at[to])
        left(dkv_send.at[0, to], kvsend.at[0, to])
        left(dkv_send.at[1, to], kvsend.at[1, to])

    @pl.loop(0, Z)
    def _(i):
        to = lax.rem(z + i, Z)

        @pl.when(jnp.logical_not((dp == z) & (i == 0)))
        def _():
            left(a_v.at[to], asend.at[to])

    @pl.loop(0, 2 * X - 1)
    def _(i):
        left(d_all.at[dp], dsend.at[i])

    @pl.loop(1, Y)
    def _(j):
        left(t_send.at[j - 1], tsend.at[j - 1])

        @pl.when(later_y(j))
        def _():
            @pl.loop(0, Z)
            def _(zz):
                left(far_v.at[j - 1, zz], fsend.at[j - 1, zz])

        @pl.when(y >= j)
        def _():
            left(part_send.at[j - 1], psend.at[j - 1])

    @pl.loop(1, DP)
    def _(i):
        left(w_all.at[dp], wsend.at[i])


def solution(mesh, y_extent=4, block=2):
    dp_n, ctx_n = mesh.shape["dp"], mesh.shape["ctx"]
    z_n = ctx_n // y_extent

    def on_device(grad_out, chosen, counts, queries, keys, values, router_logit, out_weight):
        cap, width = queries.shape[1:]
        toks, model = grad_out.shape[1:]
        nq = z_n * cap
        y_n = y_extent
        cols_y = model // y_n
        cols = cols_y // z_n
        assert width == z_n * HD == dp_n * HD
        vm = pltpu.VMEM
        dma = pltpu.SemaphoreType.DMA
        scratch = [
            vm((toks, model), BF16),
            vm((width, model), BF16),
            vm((z_n, 3 * cap + 16, HD), BF16),
            vm((z_n, 3 * cap + 16, HD), BF16),
            vm((y_n - 1, z_n, 2 * cap + 16, HD), BF16),
            vm((1, 8, nq), F32),
            vm((y_n, z_n, cap, HD), BF16),
            vm((y_n, z_n, cap, HD), BF16),
            vm((z_n, cap, HD), BF16),
            vm((z_n, cap, 1), F32),
            vm((dp_n, cap, model), BF16),
            vm((z_n, cap, HD), BF16),
            vm((z_n, cap, HD), BF16),
            vm((y_n, z_n, cap, nq), F32),
            vm((y_n, z_n, cap, nq), BF16),
            vm((z_n, cap, 1), F32),
            vm((z_n, cap, HD), BF16),
            vm((z_n, cap, HD), BF16),
            vm((z_n, 8, HD), F32),
            vm((z_n, 8, HD), F32),
            vm((z_n, cap, 1), F32),
            vm((z_n, cap, 1), F32),
            vm((z_n, cap, nq), BF16),
            vm((z_n, cap, HD), F32),
            vm((z_n, cap, HD), BF16),
            vm((y_n - 1, 2, z_n, cap, HD), BF16),
            vm((y_n - 1, 2, z_n, cap, HD), BF16),
            vm((z_n, cap, HD), F32),
            vm((z_n, cap, HD), F32),
            vm((2, z_n, cap, HD), BF16),
            vm((dp_n, cap, HD), BF16),
            vm((y_n - 1, HD, cols_y), BF16),
            vm((y_n - 1, HD, cols_y), BF16),
            vm((HD, cols_y), F32),
            vm((z_n, cols, HD), BF16),
            vm((z_n, cols, HD), BF16),
            vm((dp_n, cols, HD), F32),
            dma((3, z_n)),
            dma((2,)),
            dma((z_n,)), dma((z_n,)),
            dma((y_n - 1, z_n)), dma((y_n - 1, z_n)),
            dma((z_n,)), dma((z_n,)),
            dma((dp_n,)), dma((dp_n,)),
            dma((z_n,)), dma((dp_n,)),
            dma((z_n,)), dma((z_n,)),
            dma((y_n - 1,)), dma((y_n - 1,)),
            dma((z_n,)), dma((z_n,)),
            dma((2, z_n)), dma((2, z_n)),
            dma((y_n - 1,)), dma((y_n - 1,)),
            dma((z_n,)), dma((z_n,)),
            dma((dp_n,)), dma((dp_n,)),
        ]
        hbm = pl.BlockSpec(memory_space=pl.ANY)
        vmem = pl.BlockSpec(memory_space=pltpu.VMEM)
        smem = pl.BlockSpec(memory_space=pltpu.SMEM)
        grads = jax.ShapeDtypeStruct((1, cap, width), BF16)
        return pl.pallas_call(
            functools.partial(kernel, (dp_n, y_n, z_n, cap, block)),
            out_shape=(
                grads,
                grads,
                grads,
                jax.ShapeDtypeStruct((1, cap), F32),
                jax.ShapeDtypeStruct((width, model // ctx_n), F32),
            ),
            in_specs=[hbm, vmem, smem, hbm, hbm, hbm, vmem, hbm],
            out_specs=(hbm, hbm, hbm, vmem, vmem),
            scratch_shapes=scratch,
            compiler_params=pltpu.CompilerParams(
                collective_id=0, has_side_effects=True, vmem_limit_bytes=50 * 2**20
            ),
        )(grad_out, chosen, counts, queries, keys, values, router_logit, out_weight)

    return jax.shard_map(
        on_device,
        mesh=mesh,
        in_specs=(
            P("dp", "ctx", None),
            P("dp", "ctx"),
            P("dp", "ctx"),
            P("dp", "ctx", None),
            P("dp", "ctx", None),
            P("dp", "ctx", None),
            P("dp", "ctx"),
            P(),
        ),
        out_specs=(
            P("dp", "ctx", None),
            P("dp", "ctx", None),
            P("dp", "ctx", None),
            P("dp", "ctx"),
            P(None, "ctx"),
        ),
        check_vma=False,
    )
```

```python
import functools
import math

import jax
import jax.numpy as jnp
from jax import lax
from jax.experimental import pallas as pl
from jax.experimental.pallas import tpu as pltpu
from jax.sharding import PartitionSpec as P

MESH = pl.DeviceIdType.MESH
HD = 128
CORES = 2
NEG = -1e30
F32 = jnp.float32
BF16 = jnp.bfloat16


def rows_dot(a, b):
    return lax.dot_general(a, b, (((1,), (1,)), ((), ())), preferred_element_type=F32)


def dot(a, b):
    return jnp.dot(a, b, preferred_element_type=F32)


def turned(a):
    return jnp.transpose(a.astype(F32)).astype(a.dtype)


def kernel(
    dims,
    grad_hbm, chosen_hbm, counts_hbm, q_hbm, k_hbm, v_hbm, logit_hbm, w_hbm,
    dq_hbm, dkv_hbm, dlogit_ref, dw_ref,
    chosen_ref, counts_ref, logit_ref, q_in, k_in, v_in,
    grad_v, w_v, own_v, got_v, far_v, kb_v, kc_v, vc_v, qc_v, qb_v,
    d_all, da_send, da_v, s_v, p_v, m_v, a_v, dan_v, dl_send, dl_got, c_v, delta_v,
    ds_v, dq_acc, dq_send, part_send, part_got, own_dk, own_dv, dkv_send,
    a_all, t_send, t_got, t_own, z_send, z_got, w_all,
    load_sem, send1, recv1, fsend, frecv, dasend, darecv, dsend, drecv, d2recv,
    asend, arecv, lsend, lrecv, psend, precv, qsend, qrecv, kvsend, kvrecv,
    tsend, trecv, zsend, zrecv, wsend, wrecv,
):
    DP, Y, Z, CAP, PB = dims
    X = DP // CORES
    NQ = Z * CAP
    NB = Z // PB
    BR = PB * CAP
    dp = lax.axis_index("dp")
    ctx = lax.axis_index("ctx")
    y = lax.div(ctx, Z)
    z = lax.rem(ctx, Z)
    x = lax.div(dp, CORES)
    core = lax.rem(dp, CORES)
    width = Z * HD
    model = w_v.shape[1]
    cols_y = model // Y
    cols = cols_y // Z
    scale = 1.0 / math.sqrt(HD)
    c2 = scale * math.log2(math.e)

    def at(yy, zz):
        return yy * Z + zz

    def remote(src, dst, ss, rs, to_dp, to_ctx):
        return pltpu.make_async_remote_copy(
            src_ref=src, dst_ref=dst, send_sem=ss, recv_sem=rs,
            device_id=(to_dp, to_ctx), device_id_type=MESH,
        )

    def arrived(dst, rs):
        remote(dst, dst, rs, rs, dp, ctx).wait_recv()

    def left(src, ss):
        remote(src, src, ss, ss, dp, ctx).wait_send()

    def offset(i):
        half = lax.div(i + 1, 2)
        odd = lax.rem(i, 2)
        return odd * half + (1 - odd) * lax.rem(Z - half, Z)

    def head_cols(h):
        return pl.ds(pl.multiple_of(h * HD, HD), HD)

    loads = [
        (counts_hbm, counts_ref), (chosen_hbm, chosen_ref), (logit_hbm, logit_ref),
        (k_hbm.at[0], k_in), (v_hbm.at[0], v_in), (q_hbm.at[0], q_in), (grad_hbm.at[0], grad_v), (w_hbm, w_v),
    ]

    def load(i):
        return pltpu.make_async_copy(loads[i][0], loads[i][1], load_sem.at[i])

    for i in range(len(loads)):
        load(i).start()

    barrier = pltpu.get_barrier_semaphore()

    def greet(to_dp, to_ctx):
        pl.semaphore_signal(barrier, inc=1, device_id=(to_dp, to_ctx), device_id_type=MESH)

    @pl.loop(1, Z)
    def _(i):
        greet(dp, at(y, lax.rem(z + i, Z)))

    @pl.loop(1, Y)
    def _(i):
        greet(dp, at(lax.rem(y + i, Y), z))

    @pl.loop(1, DP)
    def _(i):
        greet(lax.rem(dp + i, DP), ctx)

    @pl.loop(0, DP)
    def _(s):
        @pl.when(jnp.logical_not((s == dp) & (z == dp)))
        def _():
            greet(s, at(y, dp))

    for i in range(6):
        load(i).wait()
    count = counts_ref[...].astype(F32)
    meta = jnp.broadcast_to(count, (16, HD)).astype(BF16)
    for h in range(Z):
        cut = pl.ds(h * HD, HD)
        own_v[h, pl.ds(0, CAP), :] = k_in[:, cut]
        own_v[h, pl.ds(CAP, CAP), :] = v_in[:, cut]
        own_v[h, pl.ds(2 * CAP, 16), :] = meta
        own_v[h, pl.ds(2 * CAP + 16, CAP), :] = q_in[:, cut]

    eye = lax.broadcasted_iota(jnp.int32, (CAP, CAP), 0) == lax.broadcasted_iota(jnp.int32, (CAP, CAP), 1)

    def column(row):
        return jnp.sum(jnp.where(eye, row, 0.0), axis=1, keepdims=True)

    gate_row = jax.nn.sigmoid(logit_ref[...])
    live_col = lax.broadcasted_iota(jnp.int32, (CAP, 1), 0).astype(F32) < count
    chosen_col = column(chosen_ref[...].astype(F32))
    toks = grad_v.shape[0]
    hot = jnp.where(
        (lax.broadcasted_iota(jnp.int32, (CAP, toks), 1).astype(F32) == chosen_col) & live_col, 1.0, 0.0
    ).astype(BF16)
    gate_col = column(gate_row)
    load(6).wait()
    d_all[dp] = (gate_col * dot(hot, grad_v[...])).astype(BF16)

    pl.semaphore_wait(barrier, (Z - 1) + (Y - 1) + (DP - 1) + DP - (dp == z).astype(jnp.int32))

    @pl.loop(1, Z)
    def _(i):
        to = lax.rem(z + offset(i), Z)
        remote(own_v.at[to], got_v.at[z], send1, recv1.at[z], dp, at(y, to)).start()

    pltpu.make_async_copy(own_v.at[z], got_v.at[z], recv1.at[z]).start()

    other = x * CORES + (1 - core)
    remote(d_all.at[dp], d_all.at[dp], dsend, d2recv, other, ctx).start()

    @pl.loop(1, X)
    def _(i):
        to = lax.rem(x + i, X) * CORES + core
        remote(d_all.at[dp], d_all.at[dp], dsend, drecv.at[dp], to, ctx).start()

    load(7).wait()
    da_all = rows_dot(d_all[dp], w_v[...]).astype(BF16)
    for h in range(Z):
        da_send[h] = da_all[:, h * HD : (h + 1) * HD]

    @pl.loop(1, Z)
    def _(i):
        to = lax.rem(z + offset(i), Z)
        remote(da_send.at[to], da_v.at[z], dasend, darecv, dp, at(y, to)).start()

    pltpu.make_async_copy(da_send.at[z], da_v.at[z], darecv).start()

    lane = lax.broadcasted_iota(jnp.int32, (1, NQ), 1).astype(F32)

    def live_lanes(zz, cnt):
        base = (zz * CAP).astype(F32)
        return (lane >= base) & (lane - base < cnt)

    def later_y(i):
        return y + i < Y

    def step(i, kb):
        frm = lax.rem(z + Z - offset(i), Z)
        arrived(got_v.at[frm], recv1.at[frm])

        @pl.loop(1, Y)
        def _(j):
            @pl.when(later_y(j))
            def _():
                kv = pl.ds(0, 2 * CAP + 16)
                remote(
                    got_v.at[frm, kv], far_v.at[j - 1, frm], fsend.at[j - 1], frecv.at[j - 1], dp, at(y + j, z)
                ).start()

        kc_v[0, frm] = got_v[frm, pl.ds(0, CAP), :]
        vc_v[0, frm] = got_v[frm, pl.ds(CAP, CAP), :]
        qc_v[frm] = got_v[frm, pl.ds(2 * CAP + 16, CAP), :]
        cnt = got_v[frm, pl.ds(2 * CAP, 16), :].astype(F32)[0:1, 0:1]
        rows = lax.broadcasted_iota(jnp.int32, (CAP, 1), 0).astype(F32)
        qb_v[frm] = jnp.where(rows < cnt, 0.0, NEG)
        return jnp.where(live_lanes(frm, cnt), 0.0, kb)

    kb0 = lax.fori_loop(0, Z, step, jnp.full((1, NQ), NEG, F32))
    kb_v[0] = jnp.broadcast_to(kb0, (8, NQ))

    def flat(a):
        return a.reshape(a.shape[0] * a.shape[1], a.shape[2])

    def blocks(a):
        return a.reshape(PB, CAP, a.shape[1])

    @pl.loop(0, NB)
    def _(b):
        some = pl.ds(b * PB, PB)
        s = rows_dot(flat(qc_v[some]), flat(kc_v[0]))
        qb = flat(qb_v[some])
        row = lax.broadcasted_iota(jnp.int32, (BR, NQ), 0) + b * BR
        col = lax.broadcasted_iota(jnp.int32, (BR, NQ), 1)
        masked = jnp.where(col < row, s + kb_v[0, 0:1, :] + qb, NEG)
        s = jnp.where(col == row, s, masked)
        s_v[0, some] = blocks(s)
        m_v[some] = blocks(jnp.max(s, axis=1, keepdims=True))

    def earlier(d, _):
        arrived(far_v.at[d - 1], frecv.at[d - 1])

        def bring(zz, kb):
            kc_v[d, zz] = far_v[d - 1, zz, pl.ds(0, CAP), :]
            vc_v[d, zz] = far_v[d - 1, zz, pl.ds(CAP, CAP), :]
            cnt = far_v[d - 1, zz, pl.ds(2 * CAP, 16), :].astype(F32)[0:1, 0:1]
            return jnp.where(live_lanes(zz, cnt), 0.0, kb)

        kb = lax.fori_loop(0, Z, bring, jnp.full((1, NQ), NEG, F32))

        @pl.loop(0, NB)
        def _(b):
            some = pl.ds(b * PB, PB)
            s = rows_dot(flat(qc_v[some]), flat(kc_v[d])) + kb
            s_v[d, some] = blocks(s)
            top = jnp.max(s, axis=1, keepdims=True) + flat(qb_v[some])
            m_v[some] = blocks(jnp.maximum(flat(m_v[some]), top))

        return 0

    lax.fori_loop(1, y + 1, earlier, 0)

    @pl.loop(1, X)
    def _(i):
        frm = lax.rem(x + i, X) * CORES + core
        arrived(d_all.at[frm], drecv.at[frm])
        remote(d_all.at[frm], d_all.at[frm], dsend, d2recv, other, ctx).start()

    arrived(da_v, darecv)

    wide = lax.broadcasted_iota(jnp.int32, (CAP, HD), 0) == lax.broadcasted_iota(jnp.int32, (CAP, HD), 1)

    @pl.loop(0, NB)
    def _(b):
        some = pl.ds(b * PB, PB)
        mc = flat(m_v[some]) * c2
        qb = flat(qb_v[some])

        def one(d, carry):
            total, o = carry
            top = mc - jnp.where(d > 0, qb, 0.0)
            p = jnp.exp2(flat(s_v[d, some]) * c2 - top)
            pb = p.astype(BF16)
            p_v[d, some] = blocks(pb)
            return total + jnp.sum(p, axis=1, keepdims=True), o + dot(pb, flat(vc_v[d]))

        total, o = lax.fori_loop(0, y + 1, one, (jnp.zeros((BR, 1), F32), jnp.zeros((BR, HD), F32)))
        inv = 1.0 / total
        att = (o * inv).astype(BF16)
        a_v[some] = blocks(att)
        da = flat(da_v[some]).astype(F32)
        delta = jnp.sum(da * att.astype(F32), axis=1, keepdims=True)
        delta_v[some] = blocks(delta)
        c_v[some] = blocks(inv * scale)
        dan_v[some] = blocks((da * inv).astype(BF16))
        for k in range(PB):
            mine = delta[k * CAP : (k + 1) * CAP]
            row = jnp.sum(jnp.where(wide, mine, 0.0), axis=0, keepdims=True)
            dl_send[b * PB + k] = jnp.broadcast_to(row, (8, HD))

    @pl.loop(0, Z)
    def _(i):
        to = lax.rem(z + i, Z)

        @pl.when(jnp.logical_not((dp == z) & (i == 0)))
        def _():
            remote(a_v.at[to], a_all.at[dp], asend, arecv, z, at(y, to)).start()

        @pl.when(i > 0)
        def _():
            remote(dl_send.at[to], dl_got.at[z], lsend, lrecv, dp, at(y, to)).start()

    @pl.when(dp == z)
    def _():
        pltpu.make_async_copy(a_v.at[z], a_all.at[dp], arecv).start()

    pltpu.make_async_copy(dl_send.at[z], dl_got.at[z], lrecv).start()

    q_t = turned(flat(qc_v[...]))
    da_t = turned(flat(dan_v[...]))
    dq_acc[...] = jnp.zeros_like(dq_acc)

    def pieces(a):
        return a.reshape(Z, CAP, HD)

    def values_grad(d):
        return pieces(jnp.transpose(dot(da_t, flat(p_v[d]))))

    def keys_grad(d):
        @pl.loop(0, NB)
        def _(b):
            some = pl.ds(b * PB, PB)
            dprobs = rows_dot(flat(da_v[some]), flat(vc_v[d]))
            ds = flat(p_v[d, some]).astype(F32) * ((dprobs - flat(delta_v[some])) * flat(c_v[some]))
            ds = ds.astype(BF16)
            ds_v[some] = blocks(ds)
            dq_acc[some] += blocks(dot(ds, flat(kc_v[d])))

        return pieces(jnp.transpose(dot(q_t, flat(ds_v[...]))))

    def part_copy(d, which):
        return remote(
            part_send.at[d - 1, which], part_got.at[d - 1, which], psend.at[d - 1, which], precv.at[d - 1, which],
            dp, at(y - d, z),
        )

    def far(d):
        part_send[d - 1, 1] = values_grad(d).astype(BF16)
        part_copy(d, 1).start()
        part_send[d - 1, 0] = keys_grad(d).astype(BF16)
        part_copy(d, 0).start()

    def weight_part():
        arrived(a_all, arecv)
        arrived(d_all.at[pl.ds(0, X)], d2recv)
        a_t = turned(flat(a_all[...]))

        @pl.loop(1, Y + 1)
        def _(i):
            to = lax.rem(y + i, Y)
            t = dot(a_t, flat(d_all[:, :, pl.ds(pl.multiple_of(to * cols_y, HD), cols_y)]))

            @pl.when(i < Y)
            def _():
                t_send[i - 1] = t.astype(BF16)
                remote(t_send.at[i - 1], t_got.at[i - 1], tsend, trecv, dp, at(to, z)).start()

            @pl.when(i == Y)
            def _():
                t_own[...] = t

    def weight_columns():
        arrived(t_got, trecv)
        t_all = t_own[...]
        for i in range(Y - 1):
            t_all = t_all + t_got[i].astype(F32)
        z_send[...] = jnp.transpose(t_all).astype(BF16).reshape(Z, cols, HD)

        @pl.loop(1, Z)
        def _(i):
            to = lax.rem(z + i, Z)
            remote(z_send.at[to], z_got.at[z], zsend, zrecv, dp, at(y, to)).start()

        pltpu.make_async_copy(z_send.at[z], z_got.at[z], zrecv).start()

    def weight_tile():
        arrived(z_got, zrecv)
        tile = z_got[0].astype(F32)
        for i in range(1, Z):
            tile = tile + z_got[i].astype(F32)
        w_all[dp] = tile

        @pl.loop(1, DP)
        def _(i):
            to = lax.rem(dp + i, DP)
            remote(w_all.at[dp], w_all.at[dp], wsend, wrecv, to, ctx).start()

    @pl.loop(0, Y - 1)
    def _(i):
        @pl.when(i < y)
        def _():
            far(y - i)

        @pl.when(i == Y - 3)
        def _():
            weight_part()

    own_dv[...] = values_grad(0)
    own_dk[...] = keys_grad(0)
    dq_send[...] = dq_acc[...].astype(BF16)

    @pl.loop(1, Z)
    def _(i):
        to = lax.rem(z + i, Z)
        remote(dq_send.at[to], dq_hbm.at[0, :, head_cols(z)], qsend, qrecv, dp, at(y, to)).start()

    pltpu.make_async_copy(dq_send.at[z], dq_hbm.at[0, :, head_cols(z)], qrecv).start()
    weight_columns()

    arrived(dl_got, lrecv)
    delta_sum = dl_got[0]
    for i in range(1, Z):
        delta_sum = delta_sum + dl_got[i]
    live_row = lax.broadcasted_iota(jnp.int32, (1, CAP), 1).astype(F32) < count
    dlogit_ref[...] = jnp.where(live_row, (1.0 - gate_row) * delta_sum[0:1, 0:CAP], 0.0)

    weight_tile()

    def add(d, _):
        for which, own in ((1, own_dv), (0, own_dk)):
            arrived(part_got.at[d - 1, which], precv.at[d - 1, which])
            own[...] += part_got[d - 1, which].astype(F32)
        return 0

    lax.fori_loop(1, Y - y, add, 0)
    dkv_send[:, 0] = own_dk[...].astype(BF16)
    dkv_send[:, 1] = own_dv[...].astype(BF16)

    @pl.loop(1, Z)
    def _(i):
        to = lax.rem(z + i, Z)
        remote(dkv_send.at[to], dkv_hbm.at[:, :, head_cols(z)], kvsend, kvrecv, dp, at(y, to)).start()

    pltpu.make_async_copy(dkv_send.at[z], dkv_hbm.at[:, :, head_cols(z)], kvrecv).start()

    arrived(w_all.at[pl.ds(0, DP - 1)], wrecv)
    for h in range(DP):
        dw_ref[:, pl.ds(h * HD, HD)] = w_all[h]

    arrived(dq_hbm, qrecv)
    most = pl.ds(0, Z - 1)
    left(own_v.at[most], send1)
    left(da_send.at[most], dasend)
    left(dl_send.at[most], lsend)
    left(dq_send.at[most], qsend)
    left(z_send.at[most], zsend)
    left(t_send, tsend)
    left(w_all.at[pl.ds(0, DP - 1)], wsend)
    left(d_all.at[pl.ds(0, 2 * X - 1)], dsend)

    @pl.when(dp != z)
    def _():
        left(a_v, asend)

    @pl.when(dp == z)
    def _():
        left(a_v.at[most], asend)

    @pl.loop(1, Y)
    def _(j):
        @pl.when(later_y(j))
        def _():
            left(far_v.at[j - 1], fsend.at[j - 1])

    @pl.loop(0, y)
    def _(j):
        left(part_send.at[j, 0], psend.at[j, 0])
        left(part_send.at[j, 1], psend.at[j, 1])

    left(dkv_send.at[most], kvsend)
    arrived(dkv_hbm, kvrecv)


def hand_out(dq_in, dkv_in, dl_in, dw_in, dq_out, dk_out, dv_out, dl_out, dw_out, sem):
    moves = (
        (dq_in, dq_out), (dkv_in.at[pl.ds(0, 1)], dk_out), (dkv_in.at[pl.ds(1, 1)], dv_out), (dl_in, dl_out), (dw_in, dw_out),
    )
    copies = [pltpu.make_async_copy(src, dst, sem.at[i]) for i, (src, dst) in enumerate(moves)]
    for copy in copies:
        copy.start()
    for copy in copies:
        copy.wait()


def solution(mesh, y_extent=4, block=8):
    dp_n, ctx_n = mesh.shape["dp"], mesh.shape["ctx"]
    z_n = ctx_n // y_extent

    def on_device(grad_out, chosen, counts, queries, keys, values, router_logit, out_weight):
        cap, width = queries.shape[1:]
        toks, model = grad_out.shape[1:]
        nq = z_n * cap
        y_n = y_extent
        cols_y = model // y_n
        cols = cols_y // z_n
        assert width == z_n * HD == dp_n * HD
        vm = pltpu.VMEM
        dma = pltpu.SemaphoreType.DMA
        scratch = [
            vm((1, cap), jnp.int32),
            vm((1, 1), jnp.int32),
            vm((1, cap), F32),
            vm((cap, width), BF16),
            vm((cap, width), BF16),
            vm((cap, width), BF16),
            vm((toks, model), BF16),
            vm((width, model), BF16),
            vm((z_n, 3 * cap + 16, HD), BF16),
            vm((z_n, 3 * cap + 16, HD), BF16),
            vm((y_n - 1, z_n, 2 * cap + 16, HD), BF16),
            vm((1, 8, nq), F32),
            vm((y_n, z_n, cap, HD), BF16),
            vm((y_n, z_n, cap, HD), BF16),
            vm((z_n, cap, HD), BF16),
            vm((z_n, cap, 1), F32),
            vm((dp_n, cap, model), BF16),
            vm((z_n, cap, HD), BF16),
            vm((z_n, cap, HD), BF16),
            vm((y_n, z_n, cap, nq), F32),
            vm((y_n, z_n, cap, nq), BF16),
            vm((z_n, cap, 1), F32),
            vm((z_n, cap, HD), BF16),
            vm((z_n, cap, HD), BF16),
            vm((z_n, 8, HD), F32),
            vm((z_n, 8, HD), F32),
            vm((z_n, cap, 1), F32),
            vm((z_n, cap, 1), F32),
            vm((z_n, cap, nq), BF16),
            vm((z_n, cap, HD), F32),
            vm((z_n, cap, HD), BF16),
            vm((y_n - 1, 2, z_n, cap, HD), BF16),
            vm((y_n - 1, 2, z_n, cap, HD), BF16),
            vm((z_n, cap, HD), F32),
            vm((z_n, cap, HD), F32),
            vm((z_n, 2, cap, HD), BF16),
            vm((dp_n, cap, HD), BF16),
            vm((y_n - 1, HD, cols_y), BF16),
            vm((y_n - 1, HD, cols_y), BF16),
            vm((HD, cols_y), F32),
            vm((z_n, cols, HD), BF16),
            vm((z_n, cols, HD), BF16),
            vm((dp_n, cols, HD), F32),
            dma((8,)),
            dma, dma((z_n,)),
            dma((y_n - 1,)), dma((y_n - 1,)),
            dma, dma,
            dma, dma((dp_n,)), dma,
            dma, dma,
            dma, dma,
            dma((y_n - 1, 2)), dma((y_n - 1, 2)),
            dma, dma,
            dma, dma,
            dma, dma,
            dma, dma,
            dma, dma,
        ]
        free = pl.BlockSpec(memory_space=pl.ANY)
        hbm = pl.BlockSpec(memory_space=pltpu.HBM)
        vmem = pl.BlockSpec(memory_space=pltpu.VMEM)
        grads = jax.ShapeDtypeStruct((1, cap, width), BF16)
        results = (
            grads,
            jax.ShapeDtypeStruct((2, cap, width), BF16),
            jax.ShapeDtypeStruct((1, cap), F32),
            jax.ShapeDtypeStruct((model // ctx_n, width), F32),
        )
        parts = pl.pallas_call(
            functools.partial(kernel, (dp_n, y_n, z_n, cap, block)),
            out_shape=results,
            in_specs=[hbm] * 8,
            out_specs=(free, free, vmem, vmem),
            scratch_shapes=scratch,
            compiler_params=pltpu.CompilerParams(
                collective_id=0, has_side_effects=True, vmem_limit_bytes=60 * 2**20
            ),
        )(grad_out, chosen, counts, queries, keys, values, router_logit, out_weight)
        dq, dk, dv, dl, dw = pl.pallas_call(
            hand_out,
            out_shape=(grads, grads, grads) + results[2:],
            in_specs=[free] * 4,
            out_specs=(hbm,) * 5,
            scratch_shapes=[dma((5,))],
        )(*parts)
        return dq, dk, dv, dl, dw.T

    return jax.shard_map(
        on_device,
        mesh=mesh,
        in_specs=(
            P("dp", "ctx", None),
            P("dp", "ctx"),
            P("dp", "ctx"),
            P("dp", "ctx", None),
            P("dp", "ctx", None),
            P("dp", "ctx", None),
            P("dp", "ctx"),
            P(),
        ),
        out_specs=(
            P("dp", "ctx", None),
            P("dp", "ctx", None),
            P("dp", "ctx", None),
            P("dp", "ctx"),
            P(None, "ctx"),
        ),
        check_vma=False,
    )
```

```python
import functools
import math

import jax
import jax.numpy as jnp
from jax import lax
from jax.experimental import pallas as pl
from jax.experimental.pallas import tpu as pltpu
from jax.sharding import PartitionSpec as P

MESH = pl.DeviceIdType.MESH
HD = 128
CORES = 2
HOSTS = 2
NEG = -1e30
F32 = jnp.float32
BF16 = jnp.bfloat16


def rows_dot(a, b):
    return lax.dot_general(a, b, (((1,), (1,)), ((), ())), preferred_element_type=F32)


def dot(a, b):
    return jnp.dot(a, b, preferred_element_type=F32)


def turned(a):
    return jnp.transpose(a.astype(F32)).astype(a.dtype)


def kernel(
    dims,
    grad_hbm, chosen_hbm, counts_hbm, q_hbm, k_hbm, v_hbm, logit_hbm, w_hbm,
    dq_hbm, dkv_hbm, dlogit_ref, dw_ref,
    chosen_ref, counts_ref, logit_ref, q_in, k_in, v_in,
    grad_v, w_v, own_v, got_v, far_v, kb_v, kc_v, vc_v, qc_v, qb_v,
    d_all, da_send, da_v, s_v, p_v, m_v, a_v, dan_v, dl_send, dl_got, c_v, delta_v,
    ds_v, dq_acc, dq_send, part_send, part_got, own_dk, own_dv, dkv_send,
    a_all, t_send, t_got, t_own, z_send, z_got, w_all,
    gq_v, gda_v, st_send, st_got, gdq_send, gdq_got, gqsend, gqrecv, gdasend, gdarecv, stsend, strecv, gdqsend, gdqrecv,
    load_sem, send1, recv1, q1send, q1recv, fsend, frecv, dasend, darecv, dsend, drecv, d2recv,
    asend, arecv, lsend, lrecv, psend, precv, qsend, qrecv, kvsend, kvrecv,
    tsend, trecv, zsend, zrecv, wsend, wrecv,
):
    DP, Y, Z, CAP, PB = dims
    X = DP // CORES
    NQ = Z * CAP
    NB = Z // PB
    BR = PB * CAP
    dp = lax.axis_index("dp")
    ctx = lax.axis_index("ctx")
    y = lax.div(ctx, Z)
    z = lax.rem(ctx, Z)
    x = lax.div(dp, CORES)
    core = lax.rem(dp, CORES)
    width = Z * HD
    model = w_v.shape[1]
    cols_y = model // Y
    cols = cols_y // Z
    scale = 1.0 / math.sqrt(HD)
    c2 = scale * math.log2(math.e)

    def at(yy, zz):
        return yy * Z + zz

    def remote(src, dst, ss, rs, to_dp, to_ctx):
        return pltpu.make_async_remote_copy(
            src_ref=src, dst_ref=dst, send_sem=ss, recv_sem=rs,
            device_id=(to_dp, to_ctx), device_id_type=MESH,
        )

    def arrived(dst, rs):
        remote(dst, dst, rs, rs, dp, ctx).wait_recv()

    def left(src, ss):
        remote(src, src, ss, ss, dp, ctx).wait_send()

    def offset(i):
        half = lax.div(i + 1, 2)
        odd = lax.rem(i, 2)
        return odd * half + (1 - odd) * lax.rem(Z - half, Z)

    def head_cols(h):
        return pl.ds(pl.multiple_of(h * HD, HD), HD)

    loads = [
        (counts_hbm, counts_ref), (chosen_hbm, chosen_ref), (logit_hbm, logit_ref),
        (k_hbm.at[0], k_in), (v_hbm.at[0], v_in), (q_hbm.at[0], q_in), (grad_hbm.at[0], grad_v), (w_hbm, w_v),
    ]

    def load(i):
        return pltpu.make_async_copy(loads[i][0], loads[i][1], load_sem.at[i])

    for i in range(len(loads)):
        load(i).start()

    barrier = pltpu.get_barrier_semaphore()

    def greet(to_dp, to_ctx):
        pl.semaphore_signal(barrier, inc=1, device_id=(to_dp, to_ctx), device_id_type=MESH)

    @pl.loop(1, Z)
    def _(i):
        greet(dp, at(y, lax.rem(z + i, Z)))

    @pl.loop(1, Y)
    def _(i):
        greet(dp, at(lax.rem(y + i, Y), z))

    @pl.loop(1, DP)
    def _(i):
        greet(lax.rem(dp + i, DP), ctx)

    @pl.loop(0, DP)
    def _(s):
        @pl.when(jnp.logical_not((s == dp) & (z == dp)))
        def _():
            greet(s, at(y, dp))

    for i in range(5):
        load(i).wait()
    count = counts_ref[...].astype(F32)
    meta = jnp.broadcast_to(count, (16, HD)).astype(BF16)
    for h in range(Z):
        cut = pl.ds(h * HD, HD)
        own_v[h, pl.ds(0, CAP), :] = k_in[:, cut]
        own_v[h, pl.ds(CAP, CAP), :] = v_in[:, cut]
        own_v[h, pl.ds(2 * CAP, 16), :] = meta

    eye = lax.broadcasted_iota(jnp.int32, (CAP, CAP), 0) == lax.broadcasted_iota(jnp.int32, (CAP, CAP), 1)

    def column(row):
        return jnp.sum(jnp.where(eye, row, 0.0), axis=1, keepdims=True)

    gate_row = jax.nn.sigmoid(logit_ref[...])
    live_col = lax.broadcasted_iota(jnp.int32, (CAP, 1), 0).astype(F32) < count
    chosen_col = column(chosen_ref[...].astype(F32))
    toks = grad_v.shape[0]
    hot = jnp.where(
        (lax.broadcasted_iota(jnp.int32, (CAP, toks), 1).astype(F32) == chosen_col) & live_col, 1.0, 0.0
    ).astype(BF16)
    gate_col = column(gate_row)
    load(6).wait()
    d_all[dp] = (gate_col * dot(hot, grad_v[...])).astype(BF16)

    pl.semaphore_wait(barrier, (Z - 1) + (Y - 1) + (DP - 1) + DP - (dp == z).astype(jnp.int32))

    @pl.loop(1, Z)
    def _(i):
        to = lax.rem(z + offset(i), Z)
        remote(own_v.at[to], got_v.at[z], send1, recv1.at[z], dp, at(y, to)).start()

    pltpu.make_async_copy(own_v.at[z], got_v.at[z], recv1.at[z]).start()
    load(5).wait()

    @pl.loop(1, Z)
    def _(i):
        to = lax.rem(z + offset(i), Z)
        remote(q_in.at[:, head_cols(to)], qc_v.at[z], q1send, q1recv, dp, at(y, to)).start()

    pltpu.make_async_copy(q_in.at[:, head_cols(z)], qc_v.at[z], q1recv).start()

    other = x * CORES + (1 - core)
    remote(d_all.at[dp], d_all.at[dp], dsend, d2recv, other, ctx).start()

    @pl.loop(1, X)
    def _(i):
        to = lax.rem(x + i, X) * CORES + core
        remote(d_all.at[dp], d_all.at[dp], dsend, drecv.at[dp], to, ctx).start()

    load(7).wait()
    da_all = rows_dot(d_all[dp], w_v[...]).astype(BF16)
    for h in range(Z):
        da_send[h] = da_all[:, h * HD : (h + 1) * HD]

    @pl.loop(1, Z)
    def _(i):
        to = lax.rem(z + offset(i), Z)
        remote(da_send.at[to], da_v.at[z], dasend, darecv, dp, at(y, to)).start()

    pltpu.make_async_copy(da_send.at[z], da_v.at[z], darecv).start()

    lane = lax.broadcasted_iota(jnp.int32, (1, NQ), 1).astype(F32)

    def live_lanes(zz, cnt):
        base = (zz * CAP).astype(F32)
        return (lane >= base) & (lane - base < cnt)

    def later_y(i):
        return y + i < Y

    def step(i, kb):
        frm = lax.rem(z + Z - offset(i), Z)
        arrived(got_v.at[frm], recv1.at[frm])

        @pl.loop(1, Y)
        def _(j):
            @pl.when(later_y(j))
            def _():
                remote(
                    got_v.at[frm], far_v.at[j - 1, frm], fsend.at[j - 1], frecv.at[j - 1], dp, at(y + j, z)
                ).start()

        kc_v[0, frm] = got_v[frm, pl.ds(0, CAP), :]
        vc_v[0, frm] = got_v[frm, pl.ds(CAP, CAP), :]
        cnt = got_v[frm, pl.ds(2 * CAP, 16), :].astype(F32)[0:1, 0:1]
        rows = lax.broadcasted_iota(jnp.int32, (CAP, 1), 0).astype(F32)
        qb_v[frm] = jnp.where(rows < cnt, 0.0, NEG)
        return jnp.where(live_lanes(frm, cnt), 0.0, kb)

    kb0 = lax.fori_loop(0, Z, step, jnp.full((1, NQ), NEG, F32))
    kb_v[0] = jnp.broadcast_to(kb0, (8, NQ))

    arrived(qc_v, q1recv)

    def to_hosts(src, dst, ss, rs):
        @pl.when(y == Y - 1)
        def _():
            for host in range(HOSTS):
                remote(src, dst, ss.at[host], rs, dp, at(host, z)).start()

    to_hosts(qc_v, gq_v, gqsend, gqrecv)

    def flat(a):
        return a.reshape(a.shape[0] * a.shape[1], a.shape[2])

    def blocks(a):
        return a.reshape(PB, CAP, a.shape[1])

    @pl.loop(0, NB)
    def _(b):
        some = pl.ds(b * PB, PB)
        s = rows_dot(flat(qc_v[some]), flat(kc_v[0]))
        qb = flat(qb_v[some])
        row = lax.broadcasted_iota(jnp.int32, (BR, NQ), 0) + b * BR
        col = lax.broadcasted_iota(jnp.int32, (BR, NQ), 1)
        masked = jnp.where(col < row, s + kb_v[0, 0:1, :] + qb, NEG)
        s = jnp.where(col == row, s, masked)
        s_v[0, some] = blocks(s)
        m_v[some] = blocks(jnp.max(s, axis=1, keepdims=True))

    def earlier(d, _):
        arrived(far_v.at[d - 1], frecv.at[d - 1])

        def bring(zz, kb):
            kc_v[d, zz] = far_v[d - 1, zz, pl.ds(0, CAP), :]
            vc_v[d, zz] = far_v[d - 1, zz, pl.ds(CAP, CAP), :]
            cnt = far_v[d - 1, zz, pl.ds(2 * CAP, 16), :].astype(F32)[0:1, 0:1]
            return jnp.where(live_lanes(zz, cnt), 0.0, kb)

        kb = lax.fori_loop(0, Z, bring, jnp.full((1, NQ), NEG, F32))

        @pl.loop(0, NB)
        def _(b):
            some = pl.ds(b * PB, PB)
            s = rows_dot(flat(qc_v[some]), flat(kc_v[d])) + kb
            s_v[d, some] = blocks(s)
            top = jnp.max(s, axis=1, keepdims=True) + flat(qb_v[some])
            m_v[some] = blocks(jnp.maximum(flat(m_v[some]), top))

        return 0

    lax.fori_loop(1, y + 1, earlier, 0)

    arrived(da_v, darecv)
    to_hosts(da_v, gda_v, gdasend, gdarecv)

    wide = lax.broadcasted_iota(jnp.int32, (CAP, HD), 0) == lax.broadcasted_iota(jnp.int32, (CAP, HD), 1)

    @pl.loop(0, NB)
    def _(b):
        some = pl.ds(b * PB, PB)
        mc = flat(m_v[some]) * c2
        qb = flat(qb_v[some])

        def one(d, carry):
            total, o = carry
            top = mc - jnp.where(d > 0, qb, 0.0)
            p = jnp.exp2(flat(s_v[d, some]) * c2 - top)
            pb = p.astype(BF16)
            p_v[d, some] = blocks(pb)
            return total + jnp.sum(p, axis=1, keepdims=True), o + dot(pb, flat(vc_v[d]))

        total, o = lax.fori_loop(0, y + 1, one, (jnp.zeros((BR, 1), F32), jnp.zeros((BR, HD), F32)))
        inv = 1.0 / total
        att = (o * inv).astype(BF16)
        a_v[some] = blocks(att)
        da = flat(da_v[some]).astype(F32)
        delta = jnp.sum(da * att.astype(F32), axis=1, keepdims=True)
        delta_v[some] = blocks(delta)
        c_v[some] = blocks(inv * scale)
        dan_v[some] = blocks((da * inv).astype(BF16))

        @pl.when(y == Y - 1)
        def _():
            which = lax.broadcasted_iota(jnp.int32, (BR, HD), 1)
            figures = jnp.where(which == 0, mc - qb, jnp.where(which == 1, delta, inv * scale))
            st_send[...] = jnp.transpose(figures)[0:8]

        for k in range(PB):
            mine = delta[k * CAP : (k + 1) * CAP]
            row = jnp.sum(jnp.where(wide, mine, 0.0), axis=0, keepdims=True)
            dl_send[b * PB + k] = jnp.broadcast_to(row, (8, HD))

    to_hosts(st_send, st_got, stsend, strecv)

    @pl.loop(0, Z)
    def _(i):
        to = lax.rem(z + i, Z)

        @pl.when(jnp.logical_not((dp == z) & (i == 0)))
        def _():
            remote(a_v.at[to], a_all.at[dp], asend, arecv, z, at(y, to)).start()

        @pl.when(i > 0)
        def _():
            remote(dl_send.at[to], dl_got.at[z], lsend, lrecv, dp, at(y, to)).start()

    @pl.when(dp == z)
    def _():
        pltpu.make_async_copy(a_v.at[z], a_all.at[dp], arecv).start()

    pltpu.make_async_copy(dl_send.at[z], dl_got.at[z], lrecv).start()

    @pl.loop(1, X)
    def _(i):
        frm = lax.rem(x + i, X) * CORES + core
        arrived(d_all.at[frm], drecv.at[frm])
        remote(d_all.at[frm], d_all.at[frm], dsend, d2recv, other, ctx).start()

    q_t = turned(flat(qc_v[...]))
    da_t = turned(flat(dan_v[...]))
    dq_acc[...] = jnp.zeros_like(dq_acc)

    def pieces(a):
        return a.reshape(Z, CAP, HD)

    def values_grad(d):
        return pieces(jnp.transpose(dot(da_t, flat(p_v[d]))))

    def keys_grad(d):
        @pl.loop(0, NB)
        def _(b):
            some = pl.ds(b * PB, PB)
            dprobs = rows_dot(flat(da_v[some]), flat(vc_v[d]))
            ds = flat(p_v[d, some]).astype(F32) * ((dprobs - flat(delta_v[some])) * flat(c_v[some]))
            ds = ds.astype(BF16)
            ds_v[some] = blocks(ds)
            dq_acc[some] += blocks(dot(ds, flat(kc_v[d])))

        return pieces(jnp.transpose(dot(q_t, flat(ds_v[...]))))

    def part_copy(d, which):
        return remote(
            part_send.at[d - 1, which], part_got.at[d - 1, which], psend.at[d - 1, which], precv.at[d - 1, which],
            dp, at(y - d, z),
        )

    def far(d):
        part_send[d - 1, 1] = values_grad(d).astype(BF16)
        part_copy(d, 1).start()
        part_send[d - 1, 0] = keys_grad(d).astype(BF16)
        part_copy(d, 0).start()

    def weight_part():
        arrived(a_all, arecv)
        arrived(d_all.at[pl.ds(0, X)], d2recv)
        a_t = turned(flat(a_all[...]))

        @pl.loop(1, Y + 1)
        def _(i):
            to = lax.rem(y + i, Y)
            t = dot(a_t, flat(d_all[:, :, pl.ds(pl.multiple_of(to * cols_y, HD), cols_y)]))

            @pl.when(i < Y)
            def _():
                t_send[i - 1] = t.astype(BF16)
                remote(t_send.at[i - 1], t_got.at[i - 1], tsend, trecv, dp, at(to, z)).start()

            @pl.when(i == Y)
            def _():
                t_own[...] = t

    def weight_columns():
        arrived(t_got, trecv)
        t_all = t_own[...]
        for i in range(Y - 1):
            t_all = t_all + t_got[i].astype(F32)
        z_send[...] = jnp.transpose(t_all).astype(BF16).reshape(Z, cols, HD)

        @pl.loop(1, Z)
        def _(i):
            to = lax.rem(z + i, Z)
            remote(z_send.at[to], z_got.at[z], zsend, zrecv, dp, at(y, to)).start()

        pltpu.make_async_copy(z_send.at[z], z_got.at[z], zrecv).start()

    def weight_tile():
        arrived(z_got, zrecv)
        tile = z_got[0].astype(F32)
        for i in range(1, Z):
            tile = tile + z_got[i].astype(F32)
        w_all[dp] = tile

        @pl.loop(1, DP)
        def _(i):
            to = lax.rem(dp + i, DP)
            remote(w_all.at[dp], w_all.at[dp], wsend, wrecv, to, ctx).start()

    def queries_out():
        dq_send[...] = dq_acc[...].astype(BF16)

        @pl.loop(1, Z)
        def _(i):
            to = lax.rem(z + i, Z)
            remote(dq_send.at[to], dq_hbm.at[0, :, head_cols(z)], qsend, qrecv, dp, at(y, to)).start()

        pltpu.make_async_copy(dq_send.at[z], dq_hbm.at[0, :, head_cols(z)], qrecv).start()

    def guest():
        arrived(gq_v, gqrecv)
        arrived(gda_v, gdarecv)
        arrived(st_got, strecv)
        figures = jnp.transpose(st_got[...])
        top, g_delta, g_c = figures[:, 0:1], figures[:, 1:2], figures[:, 2:3]
        s = rows_dot(flat(gq_v[...]), flat(kc_v[0])) + kb_v[0, 0:1, :]
        p = jnp.exp2(s * c2 - top).astype(BF16)
        p_v[Y - 1] = blocks(p)
        g_da = flat(gda_v[...])
        g_dan = (g_da.astype(F32) * (g_c * (1.0 / scale))).astype(BF16)
        own_dv[...] += pieces(jnp.transpose(dot(turned(g_dan), flat(p_v[Y - 1]))))
        dprobs = rows_dot(g_da, flat(vc_v[0]))
        ds = (flat(p_v[Y - 1]).astype(F32) * ((dprobs - g_delta) * g_c)).astype(BF16)
        ds_v[...] = blocks(ds)
        gdq_send[...] = blocks(dot(ds, flat(kc_v[0]))).astype(BF16)
        remote(gdq_send, gdq_got.at[y], gdqsend, gdqrecv.at[y], dp, at(Y - 1, z)).start()
        own_dk[...] += pieces(jnp.transpose(dot(turned(flat(gq_v[...])), flat(ds_v[...]))))

    def own():
        own_dv[...] = values_grad(0)
        own_dk[...] = keys_grad(0)

        @pl.when(y < Y - 1)
        def _():
            queries_out()

    n_far = y - HOSTS * (y == Y - 1).astype(jnp.int32)

    @pl.loop(0, Y)
    def _(i):
        @pl.when(i < n_far)
        def _():
            far(n_far - i)

        @pl.when(i == n_far)
        def _():
            own()

        @pl.when(i == 0)
        def _():
            weight_part()

        @pl.when((i == 2) & (y < HOSTS))
        def _():
            guest()

        @pl.when(i == 2)
        def _():
            weight_columns()

        @pl.when(i == 3)
        def _():
            weight_tile()

    @pl.when(y == Y - 1)
    def _():
        for host in range(HOSTS):
            arrived(gdq_got.at[host], gdqrecv.at[host])
            dq_acc[...] += gdq_got[host].astype(F32)
        queries_out()

    arrived(dl_got, lrecv)
    delta_sum = dl_got[0]
    for i in range(1, Z):
        delta_sum = delta_sum + dl_got[i]
    live_row = lax.broadcasted_iota(jnp.int32, (1, CAP), 1).astype(F32) < count
    dlogit_ref[...] = jnp.where(live_row, (1.0 - gate_row) * delta_sum[0:1, 0:CAP], 0.0)

    for which, grad in ((1, own_dv), (0, own_dk)):

        def add(d, _, which=which, grad=grad):
            arrived(part_got.at[d - 1, which], precv.at[d - 1, which])
            grad[...] += part_got[d - 1, which].astype(F32)
            return 0

        lax.fori_loop(1, Y - y - (y < HOSTS).astype(jnp.int32), add, 0)
        dkv_send[which] = grad[...].astype(BF16)

        @pl.loop(1, Z)
        def _(i, which=which):
            to = lax.rem(z + i, Z)
            remote(
                dkv_send.at[which, to], dkv_hbm.at[which, :, head_cols(z)], kvsend.at[which], kvrecv, dp, at(y, to)
            ).start()

        pltpu.make_async_copy(dkv_send.at[which, z], dkv_hbm.at[which, :, head_cols(z)], kvrecv).start()

    arrived(w_all.at[pl.ds(0, DP - 1)], wrecv)
    for h in range(DP):
        dw_ref[:, pl.ds(h * HD, HD)] = w_all[h]

    arrived(dq_hbm, qrecv)
    most = pl.ds(0, Z - 1)
    @pl.when(y == Y - 1)
    def _():
        for host in range(HOSTS):
            left(qc_v, gqsend.at[host])
            left(da_v, gdasend.at[host])
            left(st_send, stsend.at[host])

    @pl.when(y < HOSTS)
    def _():
        left(gdq_send, gdqsend)

    left(own_v.at[most], send1)
    left(qc_v.at[most], q1send)
    left(da_send.at[most], dasend)
    left(dl_send.at[most], lsend)
    left(dq_send.at[most], qsend)
    left(z_send.at[most], zsend)
    left(t_send, tsend)
    left(w_all.at[pl.ds(0, DP - 1)], wsend)
    left(d_all.at[pl.ds(0, 2 * X - 1)], dsend)

    @pl.when(dp != z)
    def _():
        left(a_v, asend)

    @pl.when(dp == z)
    def _():
        left(a_v.at[most], asend)

    @pl.loop(1, Y)
    def _(j):
        @pl.when(later_y(j))
        def _():
            left(far_v.at[j - 1], fsend.at[j - 1])

    @pl.loop(0, n_far)
    def _(j):
        left(part_send.at[j, 0], psend.at[j, 0])
        left(part_send.at[j, 1], psend.at[j, 1])

    left(dkv_send.at[0, most], kvsend.at[0])
    left(dkv_send.at[1, most], kvsend.at[1])
    arrived(dkv_hbm, kvrecv)


def hand_out(dq_in, dkv_in, dl_in, dw_in, dq_out, dk_out, dv_out, dl_out, dw_out):
    dq_out[...] = dq_in[...]
    dk_out[...] = dkv_in[pl.ds(0, 1)]
    dv_out[...] = dkv_in[pl.ds(1, 1)]
    dl_out[...] = dl_in[...]
    dw_out[...] = dw_in[...]


def solution(mesh, y_extent=4, block=8):
    dp_n, ctx_n = mesh.shape["dp"], mesh.shape["ctx"]
    z_n = ctx_n // y_extent

    def on_device(grad_out, chosen, counts, queries, keys, values, router_logit, out_weight):
        cap, width = queries.shape[1:]
        toks, model = grad_out.shape[1:]
        nq = z_n * cap
        y_n = y_extent
        cols_y = model // y_n
        cols = cols_y // z_n
        assert width == z_n * HD == dp_n * HD
        vm = pltpu.VMEM
        dma = pltpu.SemaphoreType.DMA
        scratch = [
            vm((1, cap), jnp.int32),
            vm((1, 1), jnp.int32),
            vm((1, cap), F32),
            vm((cap, width), BF16),
            vm((cap, width), BF16),
            vm((cap, width), BF16),
            vm((toks, model), BF16),
            vm((width, model), BF16),
            vm((z_n, 2 * cap + 16, HD), BF16),
            vm((z_n, 2 * cap + 16, HD), BF16),
            vm((y_n - 1, z_n, 2 * cap + 16, HD), BF16),
            vm((1, 8, nq), F32),
            vm((y_n, z_n, cap, HD), BF16),
            vm((y_n, z_n, cap, HD), BF16),
            vm((z_n, cap, HD), BF16),
            vm((z_n, cap, 1), F32),
            vm((dp_n, cap, model), BF16),
            vm((z_n, cap, HD), BF16),
            vm((z_n, cap, HD), BF16),
            vm((y_n, z_n, cap, nq), F32),
            vm((y_n, z_n, cap, nq), BF16),
            vm((z_n, cap, 1), F32),
            vm((z_n, cap, HD), BF16),
            vm((z_n, cap, HD), BF16),
            vm((z_n, 8, HD), F32),
            vm((z_n, 8, HD), F32),
            vm((z_n, cap, 1), F32),
            vm((z_n, cap, 1), F32),
            vm((z_n, cap, nq), BF16),
            vm((z_n, cap, HD), F32),
            vm((z_n, cap, HD), BF16),
            vm((y_n - 1, 2, z_n, cap, HD), BF16),
            vm((y_n - 1, 2, z_n, cap, HD), BF16),
            vm((z_n, cap, HD), F32),
            vm((z_n, cap, HD), F32),
            vm((2, z_n, cap, HD), BF16),
            vm((dp_n, cap, HD), BF16),
            vm((y_n - 1, HD, cols_y), BF16),
            vm((y_n - 1, HD, cols_y), BF16),
            vm((HD, cols_y), F32),
            vm((z_n, cols, HD), BF16),
            vm((z_n, cols, HD), BF16),
            vm((dp_n, cols, HD), F32),
            vm((z_n, cap, HD), BF16),
            vm((z_n, cap, HD), BF16),
            vm((8, nq), F32),
            vm((8, nq), F32),
            vm((z_n, cap, HD), BF16),
            vm((HOSTS, z_n, cap, HD), BF16),
            dma((HOSTS,)), dma,
            dma((HOSTS,)), dma,
            dma((HOSTS,)), dma,
            dma, dma((HOSTS,)),
            dma((8,)),
            dma, dma((z_n,)), dma, dma,
            dma((y_n - 1,)), dma((y_n - 1,)),
            dma, dma,
            dma, dma((dp_n,)), dma,
            dma, dma,
            dma, dma,
            dma((y_n - 1, 2)), dma((y_n - 1, 2)),
            dma, dma,
            dma((2,)), dma,
            dma, dma,
            dma, dma,
            dma, dma,
        ]
        free = pl.BlockSpec(memory_space=pl.ANY)
        hbm = pl.BlockSpec(memory_space=pltpu.HBM)
        vmem = pl.BlockSpec(memory_space=pltpu.VMEM)
        grads = jax.ShapeDtypeStruct((1, cap, width), BF16)
        results = (
            grads,
            jax.ShapeDtypeStruct((2, cap, width), BF16),
            jax.ShapeDtypeStruct((1, cap), F32),
            jax.ShapeDtypeStruct((model // ctx_n, width), F32),
        )
        parts = pl.pallas_call(
            functools.partial(kernel, (dp_n, y_n, z_n, cap, block)),
            out_shape=results,
            in_specs=[hbm] * 8,
            out_specs=(free, free, vmem, vmem),
            scratch_shapes=scratch,
            compiler_params=pltpu.CompilerParams(
                collective_id=0, has_side_effects=True, vmem_limit_bytes=60 * 2**20
            ),
        )(grad_out, chosen, counts, queries, keys, values, router_logit, out_weight)
        dq, dk, dv, dl, dw = pl.pallas_call(
            hand_out,
            out_shape=(grads, grads, grads) + results[2:],
            in_specs=[vmem] * 4,
            out_specs=(vmem,) * 5,
        )(*parts)
        return dq, dk, dv, dl, dw.T

    return jax.shard_map(
        on_device,
        mesh=mesh,
        in_specs=(
            P("dp", "ctx", None),
            P("dp", "ctx"),
            P("dp", "ctx"),
            P("dp", "ctx", None),
            P("dp", "ctx", None),
            P("dp", "ctx", None),
            P("dp", "ctx"),
            P(),
        ),
        out_specs=(
            P("dp", "ctx", None),
            P("dp", "ctx", None),
            P("dp", "ctx", None),
            P("dp", "ctx"),
            P(None, "ctx"),
        ),
        check_vma=False,
    )
```

```python
import functools
import math

import jax
import jax.numpy as jnp
from jax import lax
from jax.experimental import pallas as pl
from jax.experimental.pallas import tpu as pltpu
from jax.sharding import PartitionSpec as P

MESH = pl.DeviceIdType.MESH
HD = 128
CORES = 2
HOSTS = 2
NEG = -1e30
F32 = jnp.float32
BF16 = jnp.bfloat16


def rows_dot(a, b):
    return lax.dot_general(a, b, (((1,), (1,)), ((), ())), preferred_element_type=F32)


def dot(a, b):
    return jnp.dot(a, b, preferred_element_type=F32)


def turned(a):
    return jnp.transpose(a.astype(F32)).astype(a.dtype)


def kernel(
    dims,
    grad_hbm, chosen_hbm, counts_hbm, q_hbm, k_hbm, v_hbm, logit_hbm, w_hbm,
    dq_hbm, dkv_hbm, dlogit_ref, dw_ref,
    chosen_ref, counts_ref, logit_ref, q_in, k_in, v_in,
    grad_v, w_v, own_v, got_v, far_v, kb_v, kc_v, vc_v, qc_v, qb_v,
    d_all, da_send, da_v, s_v, p_v, m_v, a_v, dan_v, dl_send, dl_got, c_v, delta_v,
    ds_v, dq_acc, dq_send, part_send, part_got, own_dk, own_dv, dkv_send,
    a_all, t_send, t_got, t_own, z_send, z_got, w_all,
    gq_v, gda_v, st_send, st_got, gdq_send, gdq_got, gqsend, gqrecv, gdasend, gdarecv, stsend, strecv, gdqsend, gdqrecv,
    load_sem, send1, recv1, q1send, q1recv, fsend, frecv, dasend, darecv, dsend, drecv, d2recv,
    asend, arecv, lsend, lrecv, psend, precv, qsend, qrecv, kvsend, kvrecv,
    tsend, trecv, zsend, zrecv, wsend, wrecv,
):
    DP, Y, Z, CAP, PB = dims
    X = DP // CORES
    NQ = Z * CAP
    NB = Z // PB
    BR = PB * CAP
    dp = lax.axis_index("dp")
    ctx = lax.axis_index("ctx")
    y = lax.div(ctx, Z)
    z = lax.rem(ctx, Z)
    x = lax.div(dp, CORES)
    core = lax.rem(dp, CORES)
    width = Z * HD
    model = w_v.shape[1]
    cols_y = model // Y
    cols = cols_y // Z
    scale = 1.0 / math.sqrt(HD)
    c2 = scale * math.log2(math.e)

    def at(yy, zz):
        return yy * Z + zz

    def remote(src, dst, ss, rs, to_dp, to_ctx):
        return pltpu.make_async_remote_copy(
            src_ref=src, dst_ref=dst, send_sem=ss, recv_sem=rs,
            device_id=(to_dp, to_ctx), device_id_type=MESH,
        )

    def arrived(dst, rs):
        remote(dst, dst, rs, rs, dp, ctx).wait_recv()

    def left(src, ss):
        remote(src, src, ss, ss, dp, ctx).wait_send()

    def offset(i):
        half = lax.div(i + 1, 2)
        odd = lax.rem(i, 2)
        return odd * half + (1 - odd) * lax.rem(Z - half, Z)

    def head_cols(h):
        return pl.ds(pl.multiple_of(h * HD, HD), HD)

    loads = [
        (counts_hbm, counts_ref), (chosen_hbm, chosen_ref), (logit_hbm, logit_ref),
        (k_hbm.at[0], k_in), (v_hbm.at[0], v_in), (q_hbm.at[0], q_in), (grad_hbm.at[0], grad_v), (w_hbm, w_v),
    ]

    def load(i):
        return pltpu.make_async_copy(loads[i][0], loads[i][1], load_sem.at[i])

    for i in range(len(loads)):
        load(i).start()

    barrier = pltpu.get_barrier_semaphore()

    def greet(to_dp, to_ctx):
        pl.semaphore_signal(barrier, inc=1, device_id=(to_dp, to_ctx), device_id_type=MESH)

    @pl.loop(1, Z)
    def _(i):
        greet(dp, at(y, lax.rem(z + i, Z)))

    @pl.loop(1, Y)
    def _(i):
        greet(dp, at(lax.rem(y + i, Y), z))

    @pl.loop(1, DP)
    def _(i):
        greet(lax.rem(dp + i, DP), ctx)

    @pl.loop(0, DP)
    def _(s):
        @pl.when(jnp.logical_not((s == dp) & (z == dp)))
        def _():
            greet(s, at(y, dp))

    for i in (0, 3, 4):
        load(i).wait()
    count = counts_ref[...].astype(F32)
    meta = jnp.broadcast_to(count, (16, HD)).astype(BF16)
    for h in range(Z):
        cut = pl.ds(h * HD, HD)
        own_v[h, pl.ds(0, CAP), :] = k_in[:, cut]
        own_v[h, pl.ds(CAP, CAP), :] = v_in[:, cut]
        own_v[h, pl.ds(2 * CAP, 16), :] = meta

    pl.semaphore_wait(barrier, (Z - 1) + (Y - 1) + (DP - 1) + DP - (dp == z).astype(jnp.int32))

    @pl.loop(1, Z)
    def _(i):
        to = lax.rem(z + offset(i), Z)
        remote(own_v.at[to], got_v.at[z], send1, recv1.at[z], dp, at(y, to)).start()

    pltpu.make_async_copy(own_v.at[z], got_v.at[z], recv1.at[z]).start()
    load(5).wait()

    @pl.loop(1, Z)
    def _(i):
        to = lax.rem(z + offset(i), Z)
        remote(q_in.at[:, head_cols(to)], qc_v.at[z], q1send, q1recv, dp, at(y, to)).start()

    pltpu.make_async_copy(q_in.at[:, head_cols(z)], qc_v.at[z], q1recv).start()

    eye = lax.broadcasted_iota(jnp.int32, (CAP, CAP), 0) == lax.broadcasted_iota(jnp.int32, (CAP, CAP), 1)

    def column(row):
        return jnp.sum(jnp.where(eye, row, 0.0), axis=1, keepdims=True)

    load(1).wait()
    load(2).wait()
    gate_row = jax.nn.sigmoid(logit_ref[...])
    live_col = lax.broadcasted_iota(jnp.int32, (CAP, 1), 0).astype(F32) < count
    chosen_col = column(chosen_ref[...].astype(F32))
    toks = grad_v.shape[0]
    hot = jnp.where(
        (lax.broadcasted_iota(jnp.int32, (CAP, toks), 1).astype(F32) == chosen_col) & live_col, 1.0, 0.0
    ).astype(BF16)
    gate_col = column(gate_row)
    load(6).wait()
    d_all[dp] = (gate_col * dot(hot, grad_v[...])).astype(BF16)

    other = x * CORES + (1 - core)
    remote(d_all.at[dp], d_all.at[dp], dsend, d2recv, other, ctx).start()

    @pl.loop(1, X)
    def _(i):
        to = lax.rem(x + i, X) * CORES + core
        remote(d_all.at[dp], d_all.at[dp], dsend, drecv.at[dp], to, ctx).start()

    load(7).wait()
    da_all = rows_dot(d_all[dp], w_v[...]).astype(BF16)
    for h in range(Z):
        da_send[h] = da_all[:, h * HD : (h + 1) * HD]

    @pl.loop(1, Z)
    def _(i):
        to = lax.rem(z + offset(i), Z)
        remote(da_send.at[to], da_v.at[z], dasend, darecv, dp, at(y, to)).start()

    pltpu.make_async_copy(da_send.at[z], da_v.at[z], darecv).start()

    lane = lax.broadcasted_iota(jnp.int32, (1, NQ), 1).astype(F32)

    def live_lanes(zz, cnt):
        base = (zz * CAP).astype(F32)
        return (lane >= base) & (lane - base < cnt)

    def later_y(i):
        return y + i < Y

    def step(i, kb):
        frm = lax.rem(z + Z - offset(i), Z)
        arrived(got_v.at[frm], recv1.at[frm])

        @pl.loop(1, Y)
        def _(j):
            @pl.when(later_y(j))
            def _():
                remote(
                    got_v.at[frm], far_v.at[j - 1, frm], fsend.at[j - 1], frecv.at[j - 1], dp, at(y + j, z)
                ).start()

        kc_v[0, frm] = got_v[frm, pl.ds(0, CAP), :]
        vc_v[0, frm] = got_v[frm, pl.ds(CAP, CAP), :]
        cnt = got_v[frm, pl.ds(2 * CAP, 16), :].astype(F32)[0:1, 0:1]
        rows = lax.broadcasted_iota(jnp.int32, (CAP, 1), 0).astype(F32)
        qb_v[frm] = jnp.where(rows < cnt, 0.0, NEG)
        return jnp.where(live_lanes(frm, cnt), 0.0, kb)

    kb0 = lax.fori_loop(0, Z, step, jnp.full((1, NQ), NEG, F32))
    kb_v[0] = jnp.broadcast_to(kb0, (8, NQ))

    arrived(qc_v, q1recv)

    def to_hosts(src, dst, ss, rs):
        @pl.when(y == Y - 1)
        def _():
            for host in range(HOSTS):
                remote(src, dst, ss.at[host], rs, dp, at(host, z)).start()

    to_hosts(qc_v, gq_v, gqsend, gqrecv)

    def flat(a):
        return a.reshape(a.shape[0] * a.shape[1], a.shape[2])

    def blocks(a):
        return a.reshape(PB, CAP, a.shape[1])

    @pl.loop(0, NB)
    def _(b):
        some = pl.ds(b * PB, PB)
        s = rows_dot(flat(qc_v[some]), flat(kc_v[0]))
        qb = flat(qb_v[some])
        row = lax.broadcasted_iota(jnp.int32, (BR, NQ), 0) + b * BR
        col = lax.broadcasted_iota(jnp.int32, (BR, NQ), 1)
        masked = jnp.where(col < row, s + kb_v[0, 0:1, :] + qb, NEG)
        s = jnp.where(col == row, s, masked)
        s_v[0, some] = blocks(s)
        m_v[some] = blocks(jnp.max(s, axis=1, keepdims=True))

    def earlier(d, _):
        arrived(far_v.at[d - 1], frecv.at[d - 1])

        def bring(zz, kb):
            kc_v[d, zz] = far_v[d - 1, zz, pl.ds(0, CAP), :]
            vc_v[d, zz] = far_v[d - 1, zz, pl.ds(CAP, CAP), :]
            cnt = far_v[d - 1, zz, pl.ds(2 * CAP, 16), :].astype(F32)[0:1, 0:1]
            return jnp.where(live_lanes(zz, cnt), 0.0, kb)

        kb = lax.fori_loop(0, Z, bring, jnp.full((1, NQ), NEG, F32))

        @pl.loop(0, NB)
        def _(b):
            some = pl.ds(b * PB, PB)
            s = rows_dot(flat(qc_v[some]), flat(kc_v[d])) + kb
            s_v[d, some] = blocks(s)
            top = jnp.max(s, axis=1, keepdims=True) + flat(qb_v[some])
            m_v[some] = blocks(jnp.maximum(flat(m_v[some]), top))

        return 0

    lax.fori_loop(1, y + 1, earlier, 0)

    arrived(da_v, darecv)
    to_hosts(da_v, gda_v, gdasend, gdarecv)

    wide = lax.broadcasted_iota(jnp.int32, (CAP, HD), 0) == lax.broadcasted_iota(jnp.int32, (CAP, HD), 1)

    @pl.loop(0, NB)
    def _(b):
        some = pl.ds(b * PB, PB)
        mc = flat(m_v[some]) * c2
        qb = flat(qb_v[some])

        def one(d, carry):
            total, o = carry
            top = mc - jnp.where(d > 0, qb, 0.0)
            p = jnp.exp2(flat(s_v[d, some]) * c2 - top)
            pb = p.astype(BF16)
            p_v[d, some] = blocks(pb)
            return total + jnp.sum(p, axis=1, keepdims=True), o + dot(pb, flat(vc_v[d]))

        total, o = lax.fori_loop(0, y + 1, one, (jnp.zeros((BR, 1), F32), jnp.zeros((BR, HD), F32)))
        inv = 1.0 / total
        att = (o * inv).astype(BF16)
        a_v[some] = blocks(att)
        da = flat(da_v[some]).astype(F32)
        delta = jnp.sum(da * att.astype(F32), axis=1, keepdims=True)
        delta_v[some] = blocks(delta)
        c_v[some] = blocks(inv * scale)
        dan_v[some] = blocks((da * inv).astype(BF16))

        @pl.when(y == Y - 1)
        def _():
            which = lax.broadcasted_iota(jnp.int32, (BR, HD), 1)
            figures = jnp.where(which == 0, mc - qb, jnp.where(which == 1, delta, inv * scale))
            st_send[...] = jnp.transpose(figures)[0:8]

        for k in range(PB):
            mine = delta[k * CAP : (k + 1) * CAP]
            row = jnp.sum(jnp.where(wide, mine, 0.0), axis=0, keepdims=True)
            dl_send[b * PB + k] = jnp.broadcast_to(row, (8, HD))

    to_hosts(st_send, st_got, stsend, strecv)

    @pl.loop(0, Z)
    def _(i):
        to = lax.rem(z + i, Z)

        @pl.when(jnp.logical_not((dp == z) & (i == 0)))
        def _():
            remote(a_v.at[to], a_all.at[dp], asend, arecv, z, at(y, to)).start()

        @pl.when(i > 0)
        def _():
            remote(dl_send.at[to], dl_got.at[z], lsend, lrecv, dp, at(y, to)).start()

    @pl.when(dp == z)
    def _():
        pltpu.make_async_copy(a_v.at[z], a_all.at[dp], arecv).start()

    pltpu.make_async_copy(dl_send.at[z], dl_got.at[z], lrecv).start()

    @pl.loop(1, X)
    def _(i):
        frm = lax.rem(x + i, X) * CORES + core
        arrived(d_all.at[frm], drecv.at[frm])
        remote(d_all.at[frm], d_all.at[frm], dsend, d2recv, other, ctx).start()

    q_t = turned(flat(qc_v[...]))
    da_t = turned(flat(dan_v[...]))
    dq_acc[...] = jnp.zeros_like(dq_acc)

    def pieces(a):
        return a.reshape(Z, CAP, HD)

    def values_grad(d):
        return pieces(jnp.transpose(dot(da_t, flat(p_v[d]))))

    def keys_grad(d):
        @pl.loop(0, NB)
        def _(b):
            some = pl.ds(b * PB, PB)
            dprobs = rows_dot(flat(da_v[some]), flat(vc_v[d]))
            ds = flat(p_v[d, some]).astype(F32) * ((dprobs - flat(delta_v[some])) * flat(c_v[some]))
            ds = ds.astype(BF16)
            ds_v[some] = blocks(ds)
            dq_acc[some] += blocks(dot(ds, flat(kc_v[d])))

        return pieces(jnp.transpose(dot(q_t, flat(ds_v[...]))))

    def part_copy(d, which):
        return remote(
            part_send.at[d - 1, which], part_got.at[d - 1, which], psend.at[d - 1, which], precv.at[d - 1, which],
            dp, at(y - d, z),
        )

    def far(d):
        part_send[d - 1, 1] = values_grad(d).astype(BF16)
        part_copy(d, 1).start()
        part_send[d - 1, 0] = keys_grad(d).astype(BF16)
        part_copy(d, 0).start()

    def weight_part():
        arrived(a_all, arecv)
        arrived(d_all.at[pl.ds(0, X)], d2recv)
        a_t = turned(flat(a_all[...]))

        @pl.loop(1, Y + 1)
        def _(i):
            to = lax.rem(y + i, Y)
            t = dot(a_t, flat(d_all[:, :, pl.ds(pl.multiple_of(to * cols_y, HD), cols_y)]))

            @pl.when(i < Y)
            def _():
                t_send[i - 1] = t.astype(BF16)
                remote(t_send.at[i - 1], t_got.at[i - 1], tsend, trecv, dp, at(to, z)).start()

            @pl.when(i == Y)
            def _():
                t_own[...] = t

    def weight_columns():
        arrived(t_got, trecv)
        t_all = t_own[...]
        for i in range(Y - 1):
            t_all = t_all + t_got[i].astype(F32)
        z_send[...] = jnp.transpose(t_all).astype(BF16).reshape(Z, cols, HD)

        @pl.loop(1, Z)
        def _(i):
            to = lax.rem(z + i, Z)
            remote(z_send.at[to], z_got.at[z], zsend, zrecv, dp, at(y, to)).start()

        pltpu.make_async_copy(z_send.at[z], z_got.at[z], zrecv).start()

    def weight_tile():
        arrived(z_got, zrecv)
        tile = z_got[0].astype(F32)
        for i in range(1, Z):
            tile = tile + z_got[i].astype(F32)
        w_all[dp] = tile

        @pl.loop(1, DP)
        def _(i):
            to = lax.rem(dp + i, DP)
            remote(w_all.at[dp], w_all.at[dp], wsend, wrecv, to, ctx).start()

    def queries_out():
        dq_send[...] = dq_acc[...].astype(BF16)

        @pl.loop(1, Z)
        def _(i):
            to = lax.rem(z + i, Z)
            remote(dq_send.at[to], dq_hbm.at[0, :, head_cols(z)], qsend, qrecv, dp, at(y, to)).start()

        pltpu.make_async_copy(dq_send.at[z], dq_hbm.at[0, :, head_cols(z)], qrecv).start()

    def guest():
        arrived(gq_v, gqrecv)
        arrived(gda_v, gdarecv)
        arrived(st_got, strecv)
        figures = jnp.transpose(st_got[...])
        top, g_delta, g_c = figures[:, 0:1], figures[:, 1:2], figures[:, 2:3]
        s = rows_dot(flat(gq_v[...]), flat(kc_v[0])) + kb_v[0, 0:1, :]
        p = jnp.exp2(s * c2 - top).astype(BF16)
        p_v[Y - 1] = blocks(p)
        g_da = flat(gda_v[...])
        g_dan = (g_da.astype(F32) * (g_c * (1.0 / scale))).astype(BF16)
        own_dv[...] += pieces(jnp.transpose(dot(turned(g_dan), flat(p_v[Y - 1]))))
        dprobs = rows_dot(g_da, flat(vc_v[0]))
        ds = (flat(p_v[Y - 1]).astype(F32) * ((dprobs - g_delta) * g_c)).astype(BF16)
        ds_v[...] = blocks(ds)
        gdq_send[...] = blocks(dot(ds, flat(kc_v[0]))).astype(BF16)
        remote(gdq_send, gdq_got.at[y], gdqsend, gdqrecv.at[y], dp, at(Y - 1, z)).start()
        own_dk[...] += pieces(jnp.transpose(dot(turned(flat(gq_v[...])), flat(ds_v[...]))))

    def own():
        own_dv[...] = values_grad(0)
        own_dk[...] = keys_grad(0)

        @pl.when(y < Y - 1)
        def _():
            queries_out()

    n_far = y - HOSTS * (y == Y - 1).astype(jnp.int32)

    @pl.loop(0, Y)
    def _(i):
        @pl.when(i < n_far)
        def _():
            far(n_far - i)

        @pl.when(i == n_far)
        def _():
            own()

        @pl.when(i == 0)
        def _():
            weight_part()

        @pl.when((i == 2) & (y < HOSTS))
        def _():
            guest()

        @pl.when(i == 2)
        def _():
            weight_columns()

    for which, grad in ((1, own_dv), (0, own_dk)):

        def add(d, _, which=which, grad=grad):
            arrived(part_got.at[d - 1, which], precv.at[d - 1, which])
            grad[...] += part_got[d - 1, which].astype(F32)
            return 0

        lax.fori_loop(1, Y - y - (y < HOSTS).astype(jnp.int32), add, 0)
        dkv_send[which] = grad[...].astype(BF16)

        @pl.loop(1, Z)
        def _(i, which=which):
            to = lax.rem(z + i, Z)
            remote(
                dkv_send.at[which, to], dkv_hbm.at[which, :, head_cols(z)], kvsend.at[which], kvrecv, dp, at(y, to)
            ).start()

        pltpu.make_async_copy(dkv_send.at[which, z], dkv_hbm.at[which, :, head_cols(z)], kvrecv).start()

    @pl.when(y == Y - 1)
    def _():
        for host in range(HOSTS):
            arrived(gdq_got.at[host], gdqrecv.at[host])
            dq_acc[...] += gdq_got[host].astype(F32)
        queries_out()

    weight_tile()

    arrived(dl_got, lrecv)
    delta_sum = dl_got[0]
    for i in range(1, Z):
        delta_sum = delta_sum + dl_got[i]
    live_row = lax.broadcasted_iota(jnp.int32, (1, CAP), 1).astype(F32) < count
    dlogit_ref[...] = jnp.where(live_row, (1.0 - gate_row) * delta_sum[0:1, 0:CAP], 0.0)

    arrived(w_all.at[pl.ds(0, DP - 1)], wrecv)
    for h in range(DP):
        dw_ref[:, pl.ds(h * HD, HD)] = w_all[h]

    arrived(dq_hbm, qrecv)
    most = pl.ds(0, Z - 1)
    @pl.when(y == Y - 1)
    def _():
        for host in range(HOSTS):
            left(qc_v, gqsend.at[host])
            left(da_v, gdasend.at[host])
            left(st_send, stsend.at[host])

    @pl.when(y < HOSTS)
    def _():
        left(gdq_send, gdqsend)

    left(own_v.at[most], send1)
    left(qc_v.at[most], q1send)
    left(da_send.at[most], dasend)
    left(dl_send.at[most], lsend)
    left(dq_send.at[most], qsend)
    left(z_send.at[most], zsend)
    left(t_send, tsend)
    left(w_all.at[pl.ds(0, DP - 1)], wsend)
    left(d_all.at[pl.ds(0, 2 * X - 1)], dsend)

    @pl.when(dp != z)
    def _():
        left(a_v, asend)

    @pl.when(dp == z)
    def _():
        left(a_v.at[most], asend)

    @pl.loop(1, Y)
    def _(j):
        @pl.when(later_y(j))
        def _():
            left(far_v.at[j - 1], fsend.at[j - 1])

    @pl.loop(0, n_far)
    def _(j):
        left(part_send.at[j, 0], psend.at[j, 0])
        left(part_send.at[j, 1], psend.at[j, 1])

    left(dkv_send.at[0, most], kvsend.at[0])
    left(dkv_send.at[1, most], kvsend.at[1])
    arrived(dkv_hbm, kvrecv)


def hand_out(dq_in, dkv_in, dl_in, dw_in, dq_out, dk_out, dv_out, dl_out, dw_out):
    dq_out[...] = dq_in[...]
    dk_out[...] = dkv_in[pl.ds(0, 1)]
    dv_out[...] = dkv_in[pl.ds(1, 1)]
    dl_out[...] = dl_in[...]
    dw_out[...] = dw_in[...]


def solution(mesh, y_extent=4, block=8):
    dp_n, ctx_n = mesh.shape["dp"], mesh.shape["ctx"]
    z_n = ctx_n // y_extent

    def on_device(grad_out, chosen, counts, queries, keys, values, router_logit, out_weight):
        cap, width = queries.shape[1:]
        toks, model = grad_out.shape[1:]
        nq = z_n * cap
        y_n = y_extent
        cols_y = model // y_n
        cols = cols_y // z_n
        assert width == z_n * HD == dp_n * HD
        vm = pltpu.VMEM
        dma = pltpu.SemaphoreType.DMA
        scratch = [
            vm((1, cap), jnp.int32),
            vm((1, 1), jnp.int32),
            vm((1, cap), F32),
            vm((cap, width), BF16),
            vm((cap, width), BF16),
            vm((cap, width), BF16),
            vm((toks, model), BF16),
            vm((width, model), BF16),
            vm((z_n, 2 * cap + 16, HD), BF16),
            vm((z_n, 2 * cap + 16, HD), BF16),
            vm((y_n - 1, z_n, 2 * cap + 16, HD), BF16),
            vm((1, 8, nq), F32),
            vm((y_n, z_n, cap, HD), BF16),
            vm((y_n, z_n, cap, HD), BF16),
            vm((z_n, cap, HD), BF16),
            vm((z_n, cap, 1), F32),
            vm((dp_n, cap, model), BF16),
            vm((z_n, cap, HD), BF16),
            vm((z_n, cap, HD), BF16),
            vm((y_n, z_n, cap, nq), F32),
            vm((y_n, z_n, cap, nq), BF16),
            vm((z_n, cap, 1), F32),
            vm((z_n, cap, HD), BF16),
            vm((z_n, cap, HD), BF16),
            vm((z_n, 8, HD), F32),
            vm((z_n, 8, HD), F32),
            vm((z_n, cap, 1), F32),
            vm((z_n, cap, 1), F32),
            vm((z_n, cap, nq), BF16),
            vm((z_n, cap, HD), F32),
            vm((z_n, cap, HD), BF16),
            vm((y_n - 1, 2, z_n, cap, HD), BF16),
            vm((y_n - 1, 2, z_n, cap, HD), BF16),
            vm((z_n, cap, HD), F32),
            vm((z_n, cap, HD), F32),
            vm((2, z_n, cap, HD), BF16),
            vm((dp_n, cap, HD), BF16),
            vm((y_n - 1, HD, cols_y), BF16),
            vm((y_n - 1, HD, cols_y), BF16),
            vm((HD, cols_y), F32),
            vm((z_n, cols, HD), BF16),
            vm((z_n, cols, HD), BF16),
            vm((dp_n, cols, HD), F32),
            vm((z_n, cap, HD), BF16),
            vm((z_n, cap, HD), BF16),
            vm((8, nq), F32),
            vm((8, nq), F32),
            vm((z_n, cap, HD), BF16),
            vm((HOSTS, z_n, cap, HD), BF16),
            dma((HOSTS,)), dma,
            dma((HOSTS,)), dma,
            dma((HOSTS,)), dma,
            dma, dma((HOSTS,)),
            dma((8,)),
            dma, dma((z_n,)), dma, dma,
            dma((y_n - 1,)), dma((y_n - 1,)),
            dma, dma,
            dma, dma((dp_n,)), dma,
            dma, dma,
            dma, dma,
            dma((y_n - 1, 2)), dma((y_n - 1, 2)),
            dma, dma,
            dma((2,)), dma,
            dma, dma,
            dma, dma,
            dma, dma,
        ]
        free = pl.BlockSpec(memory_space=pl.ANY)
        hbm = pl.BlockSpec(memory_space=pltpu.HBM)
        vmem = pl.BlockSpec(memory_space=pltpu.VMEM)
        grads = jax.ShapeDtypeStruct((1, cap, width), BF16)
        results = (
            grads,
            jax.ShapeDtypeStruct((2, cap, width), BF16),
            jax.ShapeDtypeStruct((1, cap), F32),
            jax.ShapeDtypeStruct((model // ctx_n, width), F32),
        )
        parts = pl.pallas_call(
            functools.partial(kernel, (dp_n, y_n, z_n, cap, block)),
            out_shape=results,
            in_specs=[hbm] * 8,
            out_specs=(free, free, vmem, vmem),
            scratch_shapes=scratch,
            compiler_params=pltpu.CompilerParams(
                collective_id=0, has_side_effects=True, vmem_limit_bytes=60 * 2**20
            ),
        )(grad_out, chosen, counts, queries, keys, values, router_logit, out_weight)
        dq, dk, dv, dl, dw = pl.pallas_call(
            hand_out,
            out_shape=(grads, grads, grads) + results[2:],
            in_specs=[vmem] * 4,
            out_specs=(vmem,) * 5,
        )(*parts)
        return dq, dk, dv, dl, dw.T

    return jax.shard_map(
        on_device,
        mesh=mesh,
        in_specs=(
            P("dp", "ctx", None),
            P("dp", "ctx"),
            P("dp", "ctx"),
            P("dp", "ctx", None),
            P("dp", "ctx", None),
            P("dp", "ctx", None),
            P("dp", "ctx"),
            P(),
        ),
        out_specs=(
            P("dp", "ctx", None),
            P("dp", "ctx", None),
            P("dp", "ctx", None),
            P("dp", "ctx"),
            P(None, "ctx"),
        ),
        check_vma=False,
    )
```

```python
import functools
import math

import jax
import jax.numpy as jnp
from jax import lax
from jax.experimental import pallas as pl
from jax.experimental.pallas import tpu as pltpu
from jax.sharding import PartitionSpec as P

MESH = pl.DeviceIdType.MESH
HD = 128
CORES = 2
HOSTS = 2
NEG = -1e30
F32 = jnp.float32
BF16 = jnp.bfloat16


def rows_dot(a, b):
    return lax.dot_general(a, b, (((1,), (1,)), ((), ())), preferred_element_type=F32)


def dot(a, b):
    return jnp.dot(a, b, preferred_element_type=F32)


def turned(a):
    return jnp.transpose(a.astype(F32)).astype(a.dtype)


def kernel(
    dims,
    grad_hbm, chosen_hbm, counts_hbm, q_hbm, k_hbm, v_hbm, logit_hbm, w_hbm,
    dq_hbm, dkv_hbm, dlogit_ref, dw_ref,
    chosen_ref, counts_ref, logit_ref, q_in, k_in, v_in,
    grad_v, w_v, own_v, got_v, far_v, kb_v, kc_v, vc_v, qc_v, qb_v,
    d_all, da_send, da_v, s_v, p_v, m_v, a_v, dan_v, dl_send, dl_got, c_v, delta_v,
    ds_v, dq_acc, dq_send, part_send, part_got, own_dk, own_dv, dkv_send,
    a_all, t_send, t_got, t_own, z_send, z_got, w_all,
    gq_v, gda_v, st_send, st_got, gdq_send, gdq_got, gqsend, gqrecv, gdasend, gdarecv, stsend, strecv, gdqsend, gdqrecv,
    load_sem, send1, recv1, q1send, q1recv, fsend, frecv, dasend, darecv, dsend, drecv, d2recv,
    asend, arecv, lsend, lrecv, psend, precv, qsend, qrecv, kvsend, kvrecv,
    tsend, trecv, zsend, zrecv, wsend, wrecv,
):
    DP, Y, Z, CAP, PB = dims
    X = DP // CORES
    NQ = Z * CAP
    NB = Z // PB
    BR = PB * CAP
    dp = lax.axis_index("dp")
    ctx = lax.axis_index("ctx")
    y = lax.div(ctx, Z)
    z = lax.rem(ctx, Z)
    x = lax.div(dp, CORES)
    core = lax.rem(dp, CORES)
    width = Z * HD
    model = w_v.shape[1]
    cols_y = model // Y
    cols = cols_y // Z
    scale = 1.0 / math.sqrt(HD)
    c2 = scale * math.log2(math.e)

    def at(yy, zz):
        return yy * Z + zz

    def remote(src, dst, ss, rs, to_dp, to_ctx):
        return pltpu.make_async_remote_copy(
            src_ref=src, dst_ref=dst, send_sem=ss, recv_sem=rs,
            device_id=(to_dp, to_ctx), device_id_type=MESH,
        )

    def arrived(dst, rs):
        remote(dst, dst, rs, rs, dp, ctx).wait_recv()

    def left(src, ss):
        remote(src, src, ss, ss, dp, ctx).wait_send()

    def offset(i):
        half = lax.div(i + 1, 2)
        odd = lax.rem(i, 2)
        return odd * half + (1 - odd) * lax.rem(Z - half, Z)

    def head_cols(h):
        return pl.ds(pl.multiple_of(h * HD, HD), HD)

    loads = [
        (counts_hbm, counts_ref), (chosen_hbm, chosen_ref), (logit_hbm, logit_ref),
        (k_hbm.at[0], k_in), (v_hbm.at[0], v_in), (q_hbm.at[0], q_in), (grad_hbm.at[0], grad_v), (w_hbm, w_v),
    ]

    def load(i):
        return pltpu.make_async_copy(loads[i][0], loads[i][1], load_sem.at[i])

    for i in range(len(loads)):
        load(i).start()

    barrier = pltpu.get_barrier_semaphore()

    def greet(to_dp, to_ctx):
        pl.semaphore_signal(barrier, inc=1, device_id=(to_dp, to_ctx), device_id_type=MESH)

    @pl.loop(1, Z)
    def _(i):
        greet(dp, at(y, lax.rem(z + i, Z)))

    @pl.loop(1, Y)
    def _(i):
        greet(dp, at(lax.rem(y + i, Y), z))

    @pl.loop(1, DP)
    def _(i):
        greet(lax.rem(dp + i, DP), ctx)

    @pl.loop(0, DP)
    def _(s):
        @pl.when(jnp.logical_not((s == dp) & (z == dp)))
        def _():
            greet(s, at(y, dp))

    for i in (0, 3, 4):
        load(i).wait()
    count = counts_ref[...].astype(F32)
    meta = jnp.broadcast_to(count, (16, HD)).astype(BF16)
    for h in range(Z):
        cut = pl.ds(h * HD, HD)
        own_v[h, pl.ds(0, CAP), :] = k_in[:, cut]
        own_v[h, pl.ds(CAP, CAP), :] = v_in[:, cut]
        own_v[h, pl.ds(2 * CAP, 16), :] = meta

    pl.semaphore_wait(barrier, (Z - 1) + (Y - 1) + (DP - 1) + DP - (dp == z).astype(jnp.int32))

    @pl.loop(1, Z)
    def _(i):
        to = lax.rem(z + offset(i), Z)
        remote(own_v.at[to], got_v.at[z], send1, recv1.at[z], dp, at(y, to)).start()

    pltpu.make_async_copy(own_v.at[z], got_v.at[z], recv1.at[z]).start()
    load(5).wait()

    @pl.loop(1, Z)
    def _(i):
        to = lax.rem(z + offset(i), Z)
        remote(q_in.at[:, head_cols(to)], qc_v.at[z], q1send, q1recv, dp, at(y, to)).start()

    pltpu.make_async_copy(q_in.at[:, head_cols(z)], qc_v.at[z], q1recv).start()

    eye = lax.broadcasted_iota(jnp.int32, (CAP, CAP), 0) == lax.broadcasted_iota(jnp.int32, (CAP, CAP), 1)

    def column(row):
        return jnp.sum(jnp.where(eye, row, 0.0), axis=1, keepdims=True)

    load(1).wait()
    load(2).wait()
    gate_row = jax.nn.sigmoid(logit_ref[...])
    live_col = lax.broadcasted_iota(jnp.int32, (CAP, 1), 0).astype(F32) < count
    chosen_col = column(chosen_ref[...].astype(F32))
    toks = grad_v.shape[0]
    hot = jnp.where(
        (lax.broadcasted_iota(jnp.int32, (CAP, toks), 1).astype(F32) == chosen_col) & live_col, 1.0, 0.0
    ).astype(BF16)
    gate_col = column(gate_row)
    load(6).wait()
    d_all[dp] = (gate_col * dot(hot, grad_v[...])).astype(BF16)

    other = x * CORES + (1 - core)
    remote(d_all.at[dp], d_all.at[dp], dsend, d2recv, other, ctx).start()

    @pl.loop(1, X)
    def _(i):
        to = lax.rem(x + i, X) * CORES + core
        remote(d_all.at[dp], d_all.at[dp], dsend, drecv.at[dp], to, ctx).start()

    load(7).wait()
    da_all = rows_dot(d_all[dp], w_v[...]).astype(BF16)
    for h in range(Z):
        da_send[h] = da_all[:, h * HD : (h + 1) * HD]

    @pl.loop(1, Z)
    def _(i):
        to = lax.rem(z + offset(i), Z)
        remote(da_send.at[to], da_v.at[z], dasend, darecv, dp, at(y, to)).start()

    pltpu.make_async_copy(da_send.at[z], da_v.at[z], darecv).start()

    lane = lax.broadcasted_iota(jnp.int32, (1, NQ), 1).astype(F32)

    def live_lanes(zz, cnt):
        base = (zz * CAP).astype(F32)
        return (lane >= base) & (lane - base < cnt)

    def later_y(i):
        return y + i < Y

    def step(i, kb):
        frm = lax.rem(z + Z - offset(i), Z)
        arrived(got_v.at[frm], recv1.at[frm])

        @pl.loop(1, Y)
        def _(j):
            @pl.when(later_y(j))
            def _():
                remote(
                    got_v.at[frm], far_v.at[j - 1, frm], fsend.at[j - 1], frecv.at[j - 1], dp, at(y + j, z)
                ).start()

        kc_v[0, frm] = got_v[frm, pl.ds(0, CAP), :]
        vc_v[0, frm] = got_v[frm, pl.ds(CAP, CAP), :]
        cnt = got_v[frm, pl.ds(2 * CAP, 16), :].astype(F32)[0:1, 0:1]
        rows = lax.broadcasted_iota(jnp.int32, (CAP, 1), 0).astype(F32)
        qb_v[frm] = jnp.where(rows < cnt, 0.0, NEG)
        return jnp.where(live_lanes(frm, cnt), 0.0, kb)

    kb0 = lax.fori_loop(0, Z, step, jnp.full((1, NQ), NEG, F32))
    kb_v[0] = jnp.broadcast_to(kb0, (8, NQ))

    arrived(qc_v, q1recv)

    def to_hosts(src, dst, ss, rs):
        @pl.when(y == Y - 1)
        def _():
            for host in range(HOSTS):
                remote(src, dst, ss.at[host], rs, dp, at(host, z)).start()

    to_hosts(qc_v, gq_v, gqsend, gqrecv)

    def flat(a):
        return a.reshape(a.shape[0] * a.shape[1], a.shape[2])

    def blocks(a):
        return a.reshape(PB, CAP, a.shape[1])

    @pl.loop(0, NB)
    def _(b):
        some = pl.ds(b * PB, PB)
        s = rows_dot(flat(qc_v[some]), flat(kc_v[0]))
        qb = flat(qb_v[some])
        row = lax.broadcasted_iota(jnp.int32, (BR, NQ), 0) + b * BR
        col = lax.broadcasted_iota(jnp.int32, (BR, NQ), 1)
        masked = jnp.where(col < row, s + kb_v[0, 0:1, :] + qb, NEG)
        s = jnp.where(col == row, s, masked)
        s_v[0, some] = blocks(s)
        m_v[some] = blocks(jnp.max(s, axis=1, keepdims=True))

    def earlier(d, _):
        arrived(far_v.at[d - 1], frecv.at[d - 1])

        def bring(zz, kb):
            kc_v[d, zz] = far_v[d - 1, zz, pl.ds(0, CAP), :]
            vc_v[d, zz] = far_v[d - 1, zz, pl.ds(CAP, CAP), :]
            cnt = far_v[d - 1, zz, pl.ds(2 * CAP, 16), :].astype(F32)[0:1, 0:1]
            return jnp.where(live_lanes(zz, cnt), 0.0, kb)

        kb = lax.fori_loop(0, Z, bring, jnp.full((1, NQ), NEG, F32))

        @pl.loop(0, NB)
        def _(b):
            some = pl.ds(b * PB, PB)
            s = rows_dot(flat(qc_v[some]), flat(kc_v[d])) + kb
            s_v[d, some] = blocks(s)
            top = jnp.max(s, axis=1, keepdims=True) + flat(qb_v[some])
            m_v[some] = blocks(jnp.maximum(flat(m_v[some]), top))

        return 0

    lax.fori_loop(1, y + 1, earlier, 0)

    arrived(da_v, darecv)
    to_hosts(da_v, gda_v, gdasend, gdarecv)

    wide = lax.broadcasted_iota(jnp.int32, (CAP, HD), 0) == lax.broadcasted_iota(jnp.int32, (CAP, HD), 1)

    @pl.loop(0, NB)
    def _(b):
        some = pl.ds(b * PB, PB)
        mc = flat(m_v[some]) * c2
        qb = flat(qb_v[some])

        def one(d, carry):
            total, o = carry
            top = mc - jnp.where(d > 0, qb, 0.0)
            p = jnp.exp2(flat(s_v[d, some]) * c2 - top)
            pb = p.astype(BF16)
            p_v[d, some] = blocks(pb)
            return total + jnp.sum(p, axis=1, keepdims=True), o + dot(pb, flat(vc_v[d]))

        total, o = lax.fori_loop(0, y + 1, one, (jnp.zeros((BR, 1), F32), jnp.zeros((BR, HD), F32)))
        inv = 1.0 / total
        att = (o * inv).astype(BF16)
        a_v[some] = blocks(att)
        da = flat(da_v[some]).astype(F32)
        delta = jnp.sum(da * att.astype(F32), axis=1, keepdims=True)
        delta_v[some] = blocks(delta)
        c_v[some] = blocks(inv * scale)
        dan_v[some] = blocks((da * inv).astype(BF16))

        @pl.when(y == Y - 1)
        def _():
            which = lax.broadcasted_iota(jnp.int32, (BR, HD), 1)
            figures = jnp.where(which == 0, mc - qb, jnp.where(which == 1, delta, inv * scale))
            st_send[...] = jnp.transpose(figures)[0:8]

        for k in range(PB):
            mine = delta[k * CAP : (k + 1) * CAP]
            row = jnp.sum(jnp.where(wide, mine, 0.0), axis=0, keepdims=True)
            dl_send[b * PB + k] = jnp.broadcast_to(row, (8, HD))

    to_hosts(st_send, st_got, stsend, strecv)

    @pl.loop(0, Z)
    def _(i):
        to = lax.rem(z + offset(lax.rem(Z - i, Z)), Z)

        @pl.when(jnp.logical_not((dp == z) & (i == 0)))
        def _():
            remote(a_v.at[to], a_all.at[dp], asend, arecv, z, at(y, to)).start()

        @pl.when(i > 0)
        def _():
            remote(dl_send.at[to], dl_got.at[z], lsend, lrecv, dp, at(y, to)).start()

    @pl.when(dp == z)
    def _():
        pltpu.make_async_copy(a_v.at[z], a_all.at[dp], arecv).start()

    pltpu.make_async_copy(dl_send.at[z], dl_got.at[z], lrecv).start()

    @pl.loop(1, X)
    def _(i):
        frm = lax.rem(x + i, X) * CORES + core
        arrived(d_all.at[frm], drecv.at[frm])
        remote(d_all.at[frm], d_all.at[frm], dsend, d2recv, other, ctx).start()

    q_t = turned(flat(qc_v[...]))
    da_t = turned(flat(dan_v[...]))
    dq_acc[...] = jnp.zeros_like(dq_acc)

    def pieces(a):
        return a.reshape(Z, CAP, HD)

    def values_grad(d):
        return pieces(jnp.transpose(dot(da_t, flat(p_v[d]))))

    def keys_grad(d):
        @pl.loop(0, NB)
        def _(b):
            some = pl.ds(b * PB, PB)
            dprobs = rows_dot(flat(da_v[some]), flat(vc_v[d]))
            ds = flat(p_v[d, some]).astype(F32) * ((dprobs - flat(delta_v[some])) * flat(c_v[some]))
            ds = ds.astype(BF16)
            ds_v[some] = blocks(ds)
            dq_acc[some] += blocks(dot(ds, flat(kc_v[d])))

        return pieces(jnp.transpose(dot(q_t, flat(ds_v[...]))))

    def part_copy(d, which):
        return remote(
            part_send.at[d - 1, which], part_got.at[d - 1, which], psend.at[d - 1, which], precv.at[d - 1, which],
            dp, at(y - d, z),
        )

    def far(d):
        part_send[d - 1, 1] = values_grad(d).astype(BF16)
        part_copy(d, 1).start()
        part_send[d - 1, 0] = keys_grad(d).astype(BF16)
        part_copy(d, 0).start()

    def weight_part():
        arrived(a_all, arecv)
        arrived(d_all.at[pl.ds(0, X)], d2recv)
        a_t = turned(flat(a_all[...]))

        @pl.loop(1, Y + 1)
        def _(i):
            to = lax.rem(y + i, Y)
            t = dot(a_t, flat(d_all[:, :, pl.ds(pl.multiple_of(to * cols_y, HD), cols_y)]))

            @pl.when(i < Y)
            def _():
                t_send[i - 1] = t.astype(BF16)
                remote(t_send.at[i - 1], t_got.at[i - 1], tsend, trecv, dp, at(to, z)).start()

            @pl.when(i == Y)
            def _():
                t_own[...] = t

    def weight_columns():
        arrived(t_got, trecv)
        t_all = t_own[...]
        for i in range(Y - 1):
            t_all = t_all + t_got[i].astype(F32)
        z_send[...] = jnp.transpose(t_all).astype(BF16).reshape(Z, cols, HD)

        @pl.loop(1, Z)
        def _(i):
            to = lax.rem(z + offset(Z - i), Z)
            remote(z_send.at[to], z_got.at[z], zsend, zrecv, dp, at(y, to)).start()

        pltpu.make_async_copy(z_send.at[z], z_got.at[z], zrecv).start()

    def weight_tile():
        arrived(z_got, zrecv)
        tile = z_got[0].astype(F32)
        for i in range(1, Z):
            tile = tile + z_got[i].astype(F32)
        w_all[dp] = tile

        @pl.loop(1, DP)
        def _(i):
            to = lax.rem(dp + i, DP)
            remote(w_all.at[dp], w_all.at[dp], wsend, wrecv, to, ctx).start()

    def queries_out():
        dq_send[...] = dq_acc[...].astype(BF16)

        @pl.loop(1, Z)
        def _(i):
            to = lax.rem(z + offset(Z - i), Z)
            remote(dq_send.at[to], dq_hbm.at[0, :, head_cols(z)], qsend, qrecv, dp, at(y, to)).start()

        pltpu.make_async_copy(dq_send.at[z], dq_hbm.at[0, :, head_cols(z)], qrecv).start()

    def guest():
        arrived(gq_v, gqrecv)
        arrived(gda_v, gdarecv)
        arrived(st_got, strecv)
        figures = jnp.transpose(st_got[...])
        top, g_delta, g_c = figures[:, 0:1], figures[:, 1:2], figures[:, 2:3]
        s = rows_dot(flat(gq_v[...]), flat(kc_v[0])) + kb_v[0, 0:1, :]
        p = jnp.exp2(s * c2 - top).astype(BF16)
        p_v[Y - 1] = blocks(p)
        g_da = flat(gda_v[...])
        g_dan = (g_da.astype(F32) * (g_c * (1.0 / scale))).astype(BF16)
        own_dv[...] += pieces(jnp.transpose(dot(turned(g_dan), flat(p_v[Y - 1]))))
        dprobs = rows_dot(g_da, flat(vc_v[0]))
        ds = (flat(p_v[Y - 1]).astype(F32) * ((dprobs - g_delta) * g_c)).astype(BF16)
        ds_v[...] = blocks(ds)
        gdq_send[...] = blocks(dot(ds, flat(kc_v[0]))).astype(BF16)
        remote(gdq_send, gdq_got.at[y], gdqsend, gdqrecv.at[y], dp, at(Y - 1, z)).start()
        own_dk[...] += pieces(jnp.transpose(dot(turned(flat(gq_v[...])), flat(ds_v[...]))))

    def own():
        own_dv[...] = values_grad(0)
        own_dk[...] = keys_grad(0)

        @pl.when(y < Y - 1)
        def _():
            queries_out()

    n_far = y - HOSTS * (y == Y - 1).astype(jnp.int32)

    @pl.loop(0, Y)
    def _(i):
        @pl.when(i < n_far)
        def _():
            far(n_far - i)

        @pl.when(i == n_far)
        def _():
            own()

        @pl.when(i == 0)
        def _():
            weight_part()

        @pl.when((i == 2) & (y < HOSTS))
        def _():
            guest()

        @pl.when(i == 2)
        def _():
            weight_columns()

    for which, grad in ((1, own_dv), (0, own_dk)):

        def add(d, _, which=which, grad=grad):
            arrived(part_got.at[d - 1, which], precv.at[d - 1, which])
            grad[...] += part_got[d - 1, which].astype(F32)
            return 0

        lax.fori_loop(1, Y - y - (y < HOSTS).astype(jnp.int32), add, 0)
        dkv_send[which] = grad[...].astype(BF16)

        @pl.loop(1, Z)
        def _(i, which=which):
            to = lax.rem(z + offset(Z - i), Z)
            remote(
                dkv_send.at[which, to], dkv_hbm.at[which, :, head_cols(z)], kvsend.at[which], kvrecv, dp, at(y, to)
            ).start()

        pltpu.make_async_copy(dkv_send.at[which, z], dkv_hbm.at[which, :, head_cols(z)], kvrecv).start()

    @pl.when(y == Y - 1)
    def _():
        for host in range(HOSTS):
            arrived(gdq_got.at[host], gdqrecv.at[host])
            dq_acc[...] += gdq_got[host].astype(F32)
        queries_out()

    weight_tile()

    arrived(dl_got, lrecv)
    delta_sum = dl_got[0]
    for i in range(1, Z):
        delta_sum = delta_sum + dl_got[i]
    live_row = lax.broadcasted_iota(jnp.int32, (1, CAP), 1).astype(F32) < count
    dlogit_ref[...] = jnp.where(live_row, (1.0 - gate_row) * delta_sum[0:1, 0:CAP], 0.0)

    arrived(w_all.at[pl.ds(0, DP - 1)], wrecv)
    for h in range(DP):
        dw_ref[:, pl.ds(h * HD, HD)] = w_all[h]

    arrived(dq_hbm, qrecv)
    most = pl.ds(0, Z - 1)
    @pl.when(y == Y - 1)
    def _():
        for host in range(HOSTS):
            left(qc_v, gqsend.at[host])
            left(da_v, gdasend.at[host])
            left(st_send, stsend.at[host])

    @pl.when(y < HOSTS)
    def _():
        left(gdq_send, gdqsend)

    left(own_v.at[most], send1)
    left(qc_v.at[most], q1send)
    left(da_send.at[most], dasend)
    left(dl_send.at[most], lsend)
    left(dq_send.at[most], qsend)
    left(z_send.at[most], zsend)
    left(t_send, tsend)
    left(w_all.at[pl.ds(0, DP - 1)], wsend)
    left(d_all.at[pl.ds(0, 2 * X - 1)], dsend)

    @pl.when(dp != z)
    def _():
        left(a_v, asend)

    @pl.when(dp == z)
    def _():
        left(a_v.at[most], asend)

    @pl.loop(1, Y)
    def _(j):
        @pl.when(later_y(j))
        def _():
            left(far_v.at[j - 1], fsend.at[j - 1])

    @pl.loop(0, n_far)
    def _(j):
        left(part_send.at[j, 0], psend.at[j, 0])
        left(part_send.at[j, 1], psend.at[j, 1])

    left(dkv_send.at[0, most], kvsend.at[0])
    left(dkv_send.at[1, most], kvsend.at[1])
    arrived(dkv_hbm, kvrecv)


def hand_out(dq_in, dkv_in, dl_in, dw_in, dq_out, dk_out, dv_out, dl_out, dw_out):
    dq_out[...] = dq_in[...]
    dk_out[...] = dkv_in[pl.ds(0, 1)]
    dv_out[...] = dkv_in[pl.ds(1, 1)]
    dl_out[...] = dl_in[...]
    dw_out[...] = dw_in[...]


def solution(mesh, y_extent=4, block=8):
    dp_n, ctx_n = mesh.shape["dp"], mesh.shape["ctx"]
    z_n = ctx_n // y_extent

    def on_device(grad_out, chosen, counts, queries, keys, values, router_logit, out_weight):
        cap, width = queries.shape[1:]
        toks, model = grad_out.shape[1:]
        nq = z_n * cap
        y_n = y_extent
        cols_y = model // y_n
        cols = cols_y // z_n
        assert width == z_n * HD == dp_n * HD
        vm = pltpu.VMEM
        dma = pltpu.SemaphoreType.DMA
        scratch = [
            vm((1, cap), jnp.int32),
            vm((1, 1), jnp.int32),
            vm((1, cap), F32),
            vm((cap, width), BF16),
            vm((cap, width), BF16),
            vm((cap, width), BF16),
            vm((toks, model), BF16),
            vm((width, model), BF16),
            vm((z_n, 2 * cap + 16, HD), BF16),
            vm((z_n, 2 * cap + 16, HD), BF16),
            vm((y_n - 1, z_n, 2 * cap + 16, HD), BF16),
            vm((1, 8, nq), F32),
            vm((y_n, z_n, cap, HD), BF16),
            vm((y_n, z_n, cap, HD), BF16),
            vm((z_n, cap, HD), BF16),
            vm((z_n, cap, 1), F32),
            vm((dp_n, cap, model), BF16),
            vm((z_n, cap, HD), BF16),
            vm((z_n, cap, HD), BF16),
            vm((y_n, z_n, cap, nq), F32),
            vm((y_n, z_n, cap, nq), BF16),
            vm((z_n, cap, 1), F32),
            vm((z_n, cap, HD), BF16),
            vm((z_n, cap, HD), BF16),
            vm((z_n, 8, HD), F32),
            vm((z_n, 8, HD), F32),
            vm((z_n, cap, 1), F32),
            vm((z_n, cap, 1), F32),
            vm((z_n, cap, nq), BF16),
            vm((z_n, cap, HD), F32),
            vm((z_n, cap, HD), BF16),
            vm((y_n - 1, 2, z_n, cap, HD), BF16),
            vm((y_n - 1, 2, z_n, cap, HD), BF16),
            vm((z_n, cap, HD), F32),
            vm((z_n, cap, HD), F32),
            vm((2, z_n, cap, HD), BF16),
            vm((dp_n, cap, HD), BF16),
            vm((y_n - 1, HD, cols_y), BF16),
            vm((y_n - 1, HD, cols_y), BF16),
            vm((HD, cols_y), F32),
            vm((z_n, cols, HD), BF16),
            vm((z_n, cols, HD), BF16),
            vm((dp_n, cols, HD), F32),
            vm((z_n, cap, HD), BF16),
            vm((z_n, cap, HD), BF16),
            vm((8, nq), F32),
            vm((8, nq), F32),
            vm((z_n, cap, HD), BF16),
            vm((HOSTS, z_n, cap, HD), BF16),
            dma((HOSTS,)), dma,
            dma((HOSTS,)), dma,
            dma((HOSTS,)), dma,
            dma, dma((HOSTS,)),
            dma((8,)),
            dma, dma((z_n,)), dma, dma,
            dma((y_n - 1,)), dma((y_n - 1,)),
            dma, dma,
            dma, dma((dp_n,)), dma,
            dma, dma,
            dma, dma,
            dma((y_n - 1, 2)), dma((y_n - 1, 2)),
            dma, dma,
            dma((2,)), dma,
            dma, dma,
            dma, dma,
            dma, dma,
        ]
        free = pl.BlockSpec(memory_space=pl.ANY)
        hbm = pl.BlockSpec(memory_space=pltpu.HBM)
        vmem = pl.BlockSpec(memory_space=pltpu.VMEM)
        grads = jax.ShapeDtypeStruct((1, cap, width), BF16)
        results = (
            grads,
            jax.ShapeDtypeStruct((2, cap, width), BF16),
            jax.ShapeDtypeStruct((1, cap), F32),
            jax.ShapeDtypeStruct((model // ctx_n, width), F32),
        )
        parts = pl.pallas_call(
            functools.partial(kernel, (dp_n, y_n, z_n, cap, block)),
            out_shape=results,
            in_specs=[hbm] * 8,
            out_specs=(free, free, vmem, vmem),
            scratch_shapes=scratch,
            compiler_params=pltpu.CompilerParams(
                collective_id=0, has_side_effects=True, vmem_limit_bytes=60 * 2**20
            ),
        )(grad_out, chosen, counts, queries, keys, values, router_logit, out_weight)
        dq, dk, dv, dl, dw = pl.pallas_call(
            hand_out,
            out_shape=(grads, grads, grads) + results[2:],
            in_specs=[vmem] * 4,
            out_specs=(vmem,) * 5,
        )(*parts)
        return dq, dk, dv, dl, dw.T

    return jax.shard_map(
        on_device,
        mesh=mesh,
        in_specs=(
            P("dp", "ctx", None),
            P("dp", "ctx"),
            P("dp", "ctx"),
            P("dp", "ctx", None),
            P("dp", "ctx", None),
            P("dp", "ctx", None),
            P("dp", "ctx"),
            P(),
        ),
        out_specs=(
            P("dp", "ctx", None),
            P("dp", "ctx", None),
            P("dp", "ctx", None),
            P("dp", "ctx"),
            P(None, "ctx"),
        ),
        check_vma=False,
    )
```

```python
import functools
import math

import jax
import jax.numpy as jnp
from jax import lax
from jax.experimental import pallas as pl
from jax.experimental.pallas import tpu as pltpu
from jax.sharding import PartitionSpec as P

MESH = pl.DeviceIdType.MESH
HD = 128
CORES = 2
HOSTS = 2
NEG = -1e30
F32 = jnp.float32
BF16 = jnp.bfloat16


def rows_dot(a, b):
    return lax.dot_general(a, b, (((1,), (1,)), ((), ())), preferred_element_type=F32)


def dot(a, b):
    return jnp.dot(a, b, preferred_element_type=F32)


def turned(a):
    return jnp.transpose(a.astype(F32)).astype(a.dtype)


def kernel(
    dims,
    grad_hbm, chosen_hbm, counts_hbm, q_hbm, k_hbm, v_hbm, logit_hbm, w_hbm,
    dq_hbm, dkv_hbm, dlogit_ref, dw_ref,
    chosen_ref, counts_ref, logit_ref, q_in, k_in, v_in,
    grad_v, w_v, own_v, got_v, far_v, kb_v, kc_v, vc_v, qc_v, qb_v,
    d_all, da_send, da_v, s_v, p_v, m_v, a_v, dan_v, dl_send, dl_got, c_v, delta_v,
    ds_v, dq_acc, dq_send, part_send, part_got, own_dk, own_dv, dkv_send,
    a_all, t_send, t_got, t_own, z_send, z_got, w_all,
    gq_v, gda_v, st_send, st_got, gdq_send, gdq_got, gqsend, gqrecv, gdasend, gdarecv, stsend, strecv, gdqsend, gdqrecv,
    load_sem, send1, recv1, q1send, q1recv, fsend, frecv, dasend, darecv, dsend, drecv, d2recv,
    asend, arecv, lsend, lrecv, psend, precv, qsend, qrecv, kvsend, kvrecv,
    tsend, trecv, zsend, zrecv, wsend, wrecv,
):
    DP, Y, Z, CAP, PB = dims
    X = DP // CORES
    NQ = Z * CAP
    NB = Z // PB
    BR = PB * CAP
    dp = lax.axis_index("dp")
    ctx = lax.axis_index("ctx")
    y = lax.div(ctx, Z)
    z = lax.rem(ctx, Z)
    x = lax.div(dp, CORES)
    core = lax.rem(dp, CORES)
    width = Z * HD
    model = w_v.shape[1]
    cols_y = model // Y
    cols = cols_y // Z
    scale = 1.0 / math.sqrt(HD)
    c2 = scale * math.log2(math.e)

    def at(yy, zz):
        return yy * Z + zz

    def remote(src, dst, ss, rs, to_dp, to_ctx):
        return pltpu.make_async_remote_copy(
            src_ref=src, dst_ref=dst, send_sem=ss, recv_sem=rs,
            device_id=(to_dp, to_ctx), device_id_type=MESH,
        )

    def arrived(dst, rs):
        remote(dst, dst, rs, rs, dp, ctx).wait_recv()

    def left(src, ss):
        remote(src, src, ss, ss, dp, ctx).wait_send()

    def offset(i):
        half = lax.div(i + 1, 2)
        odd = lax.rem(i, 2)
        return odd * half + (1 - odd) * lax.rem(Z - half, Z)

    def head_cols(h):
        return pl.ds(pl.multiple_of(h * HD, HD), HD)

    loads = [
        (counts_hbm, counts_ref), (chosen_hbm, chosen_ref), (logit_hbm, logit_ref),
        (k_hbm.at[0], k_in), (v_hbm.at[0], v_in), (q_hbm.at[0], q_in), (grad_hbm.at[0], grad_v), (w_hbm, w_v),
    ]

    def load(i):
        return pltpu.make_async_copy(loads[i][0], loads[i][1], load_sem.at[i])

    for i in range(len(loads)):
        load(i).start()

    barrier = pltpu.get_barrier_semaphore()

    def greet(to_dp, to_ctx):
        pl.semaphore_signal(barrier, inc=1, device_id=(to_dp, to_ctx), device_id_type=MESH)

    @pl.loop(1, Z)
    def _(i):
        greet(dp, at(y, lax.rem(z + i, Z)))

    @pl.loop(1, Y)
    def _(i):
        greet(dp, at(lax.rem(y + i, Y), z))

    @pl.loop(1, DP)
    def _(i):
        greet(lax.rem(dp + i, DP), ctx)

    @pl.loop(0, DP)
    def _(s):
        @pl.when(jnp.logical_not((s == dp) & (z == dp)))
        def _():
            greet(s, at(y, dp))

    for i in (0, 3, 4):
        load(i).wait()
    count = counts_ref[...].astype(F32)
    meta = jnp.broadcast_to(count, (16, HD)).astype(BF16)
    for h in range(Z):
        cut = pl.ds(h * HD, HD)
        own_v[h, pl.ds(0, CAP), :] = k_in[:, cut]
        own_v[h, pl.ds(CAP, CAP), :] = v_in[:, cut]
        own_v[h, pl.ds(2 * CAP, 16), :] = meta

    pl.semaphore_wait(barrier, (Z - 1) + (Y - 1) + (DP - 1) + DP - (dp == z).astype(jnp.int32))

    @pl.loop(1, Z)
    def _(i):
        to = lax.rem(z + offset(i), Z)
        remote(own_v.at[to], got_v.at[z], send1, recv1.at[z], dp, at(y, to)).start()

    pltpu.make_async_copy(own_v.at[z], got_v.at[z], recv1.at[z]).start()
    load(5).wait()

    @pl.loop(1, Z)
    def _(i):
        to = lax.rem(z + offset(i), Z)
        remote(q_in.at[:, head_cols(to)], qc_v.at[z], q1send, q1recv, dp, at(y, to)).start()

    pltpu.make_async_copy(q_in.at[:, head_cols(z)], qc_v.at[z], q1recv).start()

    eye = lax.broadcasted_iota(jnp.int32, (CAP, CAP), 0) == lax.broadcasted_iota(jnp.int32, (CAP, CAP), 1)

    def column(row):
        return jnp.sum(jnp.where(eye, row, 0.0), axis=1, keepdims=True)

    load(1).wait()
    load(2).wait()
    gate_row = jax.nn.sigmoid(logit_ref[...])
    live_col = lax.broadcasted_iota(jnp.int32, (CAP, 1), 0).astype(F32) < count
    chosen_col = column(chosen_ref[...].astype(F32))
    toks = grad_v.shape[0]
    hot = jnp.where(
        (lax.broadcasted_iota(jnp.int32, (CAP, toks), 1).astype(F32) == chosen_col) & live_col, 1.0, 0.0
    ).astype(BF16)
    gate_col = column(gate_row)
    load(6).wait()
    d_all[dp] = (gate_col * dot(hot, grad_v[...])).astype(BF16)

    other = x * CORES + (1 - core)
    remote(d_all.at[dp], d_all.at[dp], dsend, d2recv, other, ctx).start()

    @pl.loop(1, X)
    def _(i):
        to = lax.rem(x + i, X) * CORES + core
        remote(d_all.at[dp], d_all.at[dp], dsend, drecv.at[dp], to, ctx).start()

    load(7).wait()
    da_all = rows_dot(d_all[dp], w_v[...]).astype(BF16)
    for h in range(Z):
        da_send[h] = da_all[:, h * HD : (h + 1) * HD]

    @pl.loop(1, Z)
    def _(i):
        to = lax.rem(z + offset(i), Z)
        remote(da_send.at[to], da_v.at[z], dasend, darecv, dp, at(y, to)).start()

    pltpu.make_async_copy(da_send.at[z], da_v.at[z], darecv).start()

    lane = lax.broadcasted_iota(jnp.int32, (1, NQ), 1).astype(F32)

    def live_lanes(zz, cnt):
        base = (zz * CAP).astype(F32)
        return (lane >= base) & (lane - base < cnt)

    def later_y(i):
        return y + i < Y

    def step(i, kb):
        frm = lax.rem(z + Z - offset(i), Z)
        arrived(got_v.at[frm], recv1.at[frm])

        @pl.loop(1, Y)
        def _(j):
            @pl.when(later_y(j))
            def _():
                remote(
                    got_v.at[frm], far_v.at[j - 1, frm], fsend.at[j - 1], frecv.at[j - 1], dp, at(y + j, z)
                ).start()

        kc_v[0, frm] = got_v[frm, pl.ds(0, CAP), :]
        vc_v[0, frm] = got_v[frm, pl.ds(CAP, CAP), :]
        cnt = got_v[frm, pl.ds(2 * CAP, 16), :].astype(F32)[0:1, 0:1]
        rows = lax.broadcasted_iota(jnp.int32, (CAP, 1), 0).astype(F32)
        qb_v[frm] = jnp.where(rows < cnt, 0.0, NEG)
        return jnp.where(live_lanes(frm, cnt), 0.0, kb)

    kb0 = lax.fori_loop(0, Z, step, jnp.full((1, NQ), NEG, F32))
    kb_v[0] = jnp.broadcast_to(kb0, (8, NQ))

    arrived(qc_v, q1recv)

    def to_hosts(src, dst, ss, rs):
        @pl.when(y == Y - 1)
        def _():
            for host in range(HOSTS):
                remote(src, dst, ss.at[host], rs, dp, at(host, z)).start()

    to_hosts(qc_v, gq_v, gqsend, gqrecv)

    def flat(a):
        return a.reshape(a.shape[0] * a.shape[1], a.shape[2])

    def blocks(a):
        return a.reshape(PB, CAP, a.shape[1])

    @pl.loop(0, NB)
    def _(b):
        some = pl.ds(b * PB, PB)
        s = rows_dot(flat(qc_v[some]), flat(kc_v[0]))
        qb = flat(qb_v[some])
        row = lax.broadcasted_iota(jnp.int32, (BR, NQ), 0) + b * BR
        col = lax.broadcasted_iota(jnp.int32, (BR, NQ), 1)
        masked = jnp.where(col < row, s + kb_v[0, 0:1, :] + qb, NEG)
        s = jnp.where(col == row, s, masked)
        s_v[0, some] = blocks(s)
        m_v[some] = blocks(jnp.max(s, axis=1, keepdims=True))

    def earlier(d, _):
        arrived(far_v.at[d - 1], frecv.at[d - 1])

        def bring(zz, kb):
            kc_v[d, zz] = far_v[d - 1, zz, pl.ds(0, CAP), :]
            vc_v[d, zz] = far_v[d - 1, zz, pl.ds(CAP, CAP), :]
            cnt = far_v[d - 1, zz, pl.ds(2 * CAP, 16), :].astype(F32)[0:1, 0:1]
            return jnp.where(live_lanes(zz, cnt), 0.0, kb)

        kb = lax.fori_loop(0, Z, bring, jnp.full((1, NQ), NEG, F32))

        @pl.loop(0, NB)
        def _(b):
            some = pl.ds(b * PB, PB)
            s = rows_dot(flat(qc_v[some]), flat(kc_v[d])) + kb
            s_v[d, some] = blocks(s)
            top = jnp.max(s, axis=1, keepdims=True) + flat(qb_v[some])
            m_v[some] = blocks(jnp.maximum(flat(m_v[some]), top))

        return 0

    lax.fori_loop(1, y + 1, earlier, 0)

    arrived(da_v, darecv)
    to_hosts(da_v, gda_v, gdasend, gdarecv)

    wide = lax.broadcasted_iota(jnp.int32, (CAP, HD), 0) == lax.broadcasted_iota(jnp.int32, (CAP, HD), 1)

    @pl.loop(0, NB)
    def _(b):
        some = pl.ds(b * PB, PB)
        mc = flat(m_v[some]) * c2
        qb = flat(qb_v[some])

        def one(d, carry):
            total, o = carry
            top = mc - jnp.where(d > 0, qb, 0.0)
            p = jnp.exp2(flat(s_v[d, some]) * c2 - top)
            pb = p.astype(BF16)
            p_v[d, some] = blocks(pb)
            return total + jnp.sum(p, axis=1, keepdims=True), o + dot(pb, flat(vc_v[d]))

        total, o = lax.fori_loop(0, y + 1, one, (jnp.zeros((BR, 1), F32), jnp.zeros((BR, HD), F32)))
        inv = 1.0 / total
        att = (o * inv).astype(BF16)
        a_v[some] = blocks(att)
        da = flat(da_v[some]).astype(F32)
        delta = jnp.sum(da * att.astype(F32), axis=1, keepdims=True)
        delta_v[some] = blocks(delta)
        c_v[some] = blocks(inv * scale)
        dan_v[some] = blocks((da * inv).astype(BF16))

        @pl.when(y == Y - 1)
        def _():
            which = lax.broadcasted_iota(jnp.int32, (BR, HD), 1)
            figures = jnp.where(which == 0, mc - qb, jnp.where(which == 1, delta, inv * scale))
            st_send[...] = jnp.transpose(figures)[0:8]

        for k in range(PB):
            mine = delta[k * CAP : (k + 1) * CAP]
            row = jnp.sum(jnp.where(wide, mine, 0.0), axis=0, keepdims=True)
            dl_send[b * PB + k] = jnp.broadcast_to(row, (8, HD))

    to_hosts(st_send, st_got, stsend, strecv)

    @pl.loop(0, Z)
    def _(i):
        to = lax.rem(z + offset(lax.rem(Z - i, Z)), Z)

        @pl.when(jnp.logical_not((dp == z) & (i == 0)))
        def _():
            remote(a_v.at[to], a_all.at[dp], asend, arecv, z, at(y, to)).start()

    @pl.when(dp == z)
    def _():
        pltpu.make_async_copy(a_v.at[z], a_all.at[dp], arecv).start()

    @pl.loop(1, Z)
    def _(i):
        to = lax.rem(z + offset(Z - i), Z)
        remote(dl_send.at[to], dl_got.at[z], lsend, lrecv, dp, at(y, to)).start()

    pltpu.make_async_copy(dl_send.at[z], dl_got.at[z], lrecv).start()

    @pl.loop(1, X)
    def _(i):
        frm = lax.rem(x + i, X) * CORES + core
        arrived(d_all.at[frm], drecv.at[frm])
        remote(d_all.at[frm], d_all.at[frm], dsend, d2recv, other, ctx).start()

    q_t = turned(flat(qc_v[...]))
    da_t = turned(flat(dan_v[...]))
    dq_acc[...] = jnp.zeros_like(dq_acc)

    def pieces(a):
        return a.reshape(Z, CAP, HD)

    def values_grad(d):
        return pieces(jnp.transpose(dot(da_t, flat(p_v[d]))))

    def keys_grad(d):
        @pl.loop(0, NB)
        def _(b):
            some = pl.ds(b * PB, PB)
            dprobs = rows_dot(flat(da_v[some]), flat(vc_v[d]))
            ds = flat(p_v[d, some]).astype(F32) * ((dprobs - flat(delta_v[some])) * flat(c_v[some]))
            ds = ds.astype(BF16)
            ds_v[some] = blocks(ds)
            dq_acc[some] += blocks(dot(ds, flat(kc_v[d])))

        return pieces(jnp.transpose(dot(q_t, flat(ds_v[...]))))

    def part_copy(d, which):
        return remote(
            part_send.at[d - 1, which], part_got.at[d - 1, which], psend.at[d - 1, which], precv.at[d - 1, which],
            dp, at(y - d, z),
        )

    def far(d):
        part_send[d - 1, 1] = values_grad(d).astype(BF16)
        part_copy(d, 1).start()
        part_send[d - 1, 0] = keys_grad(d).astype(BF16)
        part_copy(d, 0).start()

    def weight_part():
        arrived(a_all, arecv)
        arrived(d_all.at[pl.ds(0, X)], d2recv)
        a_t = turned(flat(a_all[...]))

        @pl.loop(1, Y + 1)
        def _(i):
            to = lax.rem(y + i, Y)
            t = dot(a_t, flat(d_all[:, :, pl.ds(pl.multiple_of(to * cols_y, HD), cols_y)]))

            @pl.when(i < Y)
            def _():
                t_send[i - 1] = t.astype(BF16)
                remote(t_send.at[i - 1], t_got.at[i - 1], tsend, trecv, dp, at(to, z)).start()

            @pl.when(i == Y)
            def _():
                t_own[...] = t

    def weight_columns():
        arrived(t_got, trecv)
        t_all = t_own[...]
        for i in range(Y - 1):
            t_all = t_all + t_got[i].astype(F32)
        z_send[...] = jnp.transpose(t_all).astype(BF16).reshape(Z, cols, HD)

        @pl.loop(1, Z)
        def _(i):
            to = lax.rem(z + offset(Z - i), Z)
            remote(z_send.at[to], z_got.at[z], zsend, zrecv, dp, at(y, to)).start()

        pltpu.make_async_copy(z_send.at[z], z_got.at[z], zrecv).start()

    def weight_tile():
        arrived(z_got, zrecv)
        tile = z_got[0].astype(F32)
        for i in range(1, Z):
            tile = tile + z_got[i].astype(F32)
        w_all[dp] = tile

        @pl.loop(1, DP)
        def _(i):
            to = lax.rem(dp + i, DP)
            remote(w_all.at[dp], w_all.at[dp], wsend, wrecv, to, ctx).start()

    def queries_out():
        dq_send[...] = dq_acc[...].astype(BF16)

        @pl.loop(1, Z)
        def _(i):
            to = lax.rem(z + offset(Z - i), Z)
            remote(dq_send.at[to], dq_hbm.at[0, :, head_cols(z)], qsend, qrecv, dp, at(y, to)).start()

        pltpu.make_async_copy(dq_send.at[z], dq_hbm.at[0, :, head_cols(z)], qrecv).start()

    def guest():
        arrived(gq_v, gqrecv)
        arrived(gda_v, gdarecv)
        arrived(st_got, strecv)
        figures = jnp.transpose(st_got[...])
        top, g_delta, g_c = figures[:, 0:1], figures[:, 1:2], figures[:, 2:3]
        s = rows_dot(flat(gq_v[...]), flat(kc_v[0])) + kb_v[0, 0:1, :]
        p = jnp.exp2(s * c2 - top).astype(BF16)
        p_v[Y - 1] = blocks(p)
        g_da = flat(gda_v[...])
        g_dan = (g_da.astype(F32) * (g_c * (1.0 / scale))).astype(BF16)
        own_dv[...] += pieces(jnp.transpose(dot(turned(g_dan), flat(p_v[Y - 1]))))
        dprobs = rows_dot(g_da, flat(vc_v[0]))
        ds = (flat(p_v[Y - 1]).astype(F32) * ((dprobs - g_delta) * g_c)).astype(BF16)
        ds_v[...] = blocks(ds)
        gdq_send[...] = blocks(dot(ds, flat(kc_v[0]))).astype(BF16)
        remote(gdq_send, gdq_got.at[y], gdqsend, gdqrecv.at[y], dp, at(Y - 1, z)).start()
        own_dk[...] += pieces(jnp.transpose(dot(turned(flat(gq_v[...])), flat(ds_v[...]))))

    def own():
        own_dv[...] = values_grad(0)
        own_dk[...] = keys_grad(0)

        @pl.when(y < Y - 1)
        def _():
            queries_out()

    n_far = y - HOSTS * (y == Y - 1).astype(jnp.int32)

    @pl.loop(0, Y)
    def _(i):
        @pl.when(i < n_far)
        def _():
            far(n_far - i)

        @pl.when(i == n_far)
        def _():
            own()

        @pl.when(i == 0)
        def _():
            weight_part()

        @pl.when((i == 2) & (y < HOSTS))
        def _():
            guest()

        @pl.when(i == 2)
        def _():
            weight_columns()

    for which, grad in ((1, own_dv), (0, own_dk)):

        def add(d, _, which=which, grad=grad):
            arrived(part_got.at[d - 1, which], precv.at[d - 1, which])
            grad[...] += part_got[d - 1, which].astype(F32)
            return 0

        lax.fori_loop(1, Y - y - (y < HOSTS).astype(jnp.int32), add, 0)
        dkv_send[which] = grad[...].astype(BF16)

        @pl.loop(1, Z)
        def _(i, which=which):
            to = lax.rem(z + offset(Z - i), Z)
            remote(
                dkv_send.at[which, to], dkv_hbm.at[which, :, head_cols(z)], kvsend.at[which], kvrecv, dp, at(y, to)
            ).start()

        pltpu.make_async_copy(dkv_send.at[which, z], dkv_hbm.at[which, :, head_cols(z)], kvrecv).start()

    @pl.when(y == Y - 1)
    def _():
        for host in range(HOSTS):
            arrived(gdq_got.at[host], gdqrecv.at[host])
            dq_acc[...] += gdq_got[host].astype(F32)
        queries_out()

    weight_tile()

    arrived(dl_got, lrecv)
    delta_sum = dl_got[0]
    for i in range(1, Z):
        delta_sum = delta_sum + dl_got[i]
    live_row = lax.broadcasted_iota(jnp.int32, (1, CAP), 1).astype(F32) < count
    dlogit_ref[...] = jnp.where(live_row, (1.0 - gate_row) * delta_sum[0:1, 0:CAP], 0.0)

    arrived(w_all.at[pl.ds(0, DP - 1)], wrecv)
    for h in range(DP):
        dw_ref[:, pl.ds(h * HD, HD)] = w_all[h]

    arrived(dq_hbm, qrecv)
    most = pl.ds(0, Z - 1)
    @pl.when(y == Y - 1)
    def _():
        for host in range(HOSTS):
            left(qc_v, gqsend.at[host])
            left(da_v, gdasend.at[host])
            left(st_send, stsend.at[host])

    @pl.when(y < HOSTS)
    def _():
        left(gdq_send, gdqsend)

    left(own_v.at[most], send1)
    left(qc_v.at[most], q1send)
    left(da_send.at[most], dasend)
    left(dl_send.at[most], lsend)
    left(dq_send.at[most], qsend)
    left(z_send.at[most], zsend)
    left(t_send, tsend)
    left(w_all.at[pl.ds(0, DP - 1)], wsend)
    left(d_all.at[pl.ds(0, 2 * X - 1)], dsend)

    @pl.when(dp != z)
    def _():
        left(a_v, asend)

    @pl.when(dp == z)
    def _():
        left(a_v.at[most], asend)

    @pl.loop(1, Y)
    def _(j):
        @pl.when(later_y(j))
        def _():
            left(far_v.at[j - 1], fsend.at[j - 1])

    @pl.loop(0, n_far)
    def _(j):
        left(part_send.at[j, 0], psend.at[j, 0])
        left(part_send.at[j, 1], psend.at[j, 1])

    left(dkv_send.at[0, most], kvsend.at[0])
    left(dkv_send.at[1, most], kvsend.at[1])
    arrived(dkv_hbm, kvrecv)


def hand_out(dq_in, dkv_in, dl_in, dw_in, dq_out, dk_out, dv_out, dl_out, dw_out):
    dq_out[...] = dq_in[...]
    dk_out[...] = dkv_in[pl.ds(0, 1)]
    dv_out[...] = dkv_in[pl.ds(1, 1)]
    dl_out[...] = dl_in[...]
    dw_out[...] = dw_in[...]


def solution(mesh, y_extent=4, block=8):
    dp_n, ctx_n = mesh.shape["dp"], mesh.shape["ctx"]
    z_n = ctx_n // y_extent

    def on_device(grad_out, chosen, counts, queries, keys, values, router_logit, out_weight):
        cap, width = queries.shape[1:]
        toks, model = grad_out.shape[1:]
        nq = z_n * cap
        y_n = y_extent
        cols_y = model // y_n
        cols = cols_y // z_n
        assert width == z_n * HD == dp_n * HD
        vm = pltpu.VMEM
        dma = pltpu.SemaphoreType.DMA
        scratch = [
            vm((1, cap), jnp.int32),
            vm((1, 1), jnp.int32),
            vm((1, cap), F32),
            vm((cap, width), BF16),
            vm((cap, width), BF16),
            vm((cap, width), BF16),
            vm((toks, model), BF16),
            vm((width, model), BF16),
            vm((z_n, 2 * cap + 16, HD), BF16),
            vm((z_n, 2 * cap + 16, HD), BF16),
            vm((y_n - 1, z_n, 2 * cap + 16, HD), BF16),
            vm((1, 8, nq), F32),
            vm((y_n, z_n, cap, HD), BF16),
            vm((y_n, z_n, cap, HD), BF16),
            vm((z_n, cap, HD), BF16),
            vm((z_n, cap, 1), F32),
            vm((dp_n, cap, model), BF16),
            vm((z_n, cap, HD), BF16),
            vm((z_n, cap, HD), BF16),
            vm((y_n, z_n, cap, nq), F32),
            vm((y_n, z_n, cap, nq), BF16),
            vm((z_n, cap, 1), F32),
            vm((z_n, cap, HD), BF16),
            vm((z_n, cap, HD), BF16),
            vm((z_n, 8, HD), F32),
            vm((z_n, 8, HD), F32),
            vm((z_n, cap, 1), F32),
            vm((z_n, cap, 1), F32),
            vm((z_n, cap, nq), BF16),
            vm((z_n, cap, HD), F32),
            vm((z_n, cap, HD), BF16),
            vm((y_n - 1, 2, z_n, cap, HD), BF16),
            vm((y_n - 1, 2, z_n, cap, HD), BF16),
            vm((z_n, cap, HD), F32),
            vm((z_n, cap, HD), F32),
            vm((2, z_n, cap, HD), BF16),
            vm((dp_n, cap, HD), BF16),
            vm((y_n - 1, HD, cols_y), BF16),
            vm((y_n - 1, HD, cols_y), BF16),
            vm((HD, cols_y), F32),
            vm((z_n, cols, HD), BF16),
            vm((z_n, cols, HD), BF16),
            vm((dp_n, cols, HD), F32),
            vm((z_n, cap, HD), BF16),
            vm((z_n, cap, HD), BF16),
            vm((8, nq), F32),
            vm((8, nq), F32),
            vm((z_n, cap, HD), BF16),
            vm((HOSTS, z_n, cap, HD), BF16),
            dma((HOSTS,)), dma,
            dma((HOSTS,)), dma,
            dma((HOSTS,)), dma,
            dma, dma((HOSTS,)),
            dma((8,)),
            dma, dma((z_n,)), dma, dma,
            dma((y_n - 1,)), dma((y_n - 1,)),
            dma, dma,
            dma, dma((dp_n,)), dma,
            dma, dma,
            dma, dma,
            dma((y_n - 1, 2)), dma((y_n - 1, 2)),
            dma, dma,
            dma((2,)), dma,
            dma, dma,
            dma, dma,
            dma, dma,
        ]
        free = pl.BlockSpec(memory_space=pl.ANY)
        hbm = pl.BlockSpec(memory_space=pltpu.HBM)
        vmem = pl.BlockSpec(memory_space=pltpu.VMEM)
        grads = jax.ShapeDtypeStruct((1, cap, width), BF16)
        results = (
            grads,
            jax.ShapeDtypeStruct((2, cap, width), BF16),
            jax.ShapeDtypeStruct((1, cap), F32),
            jax.ShapeDtypeStruct((model // ctx_n, width), F32),
        )
        parts = pl.pallas_call(
            functools.partial(kernel, (dp_n, y_n, z_n, cap, block)),
            out_shape=results,
            in_specs=[hbm] * 8,
            out_specs=(free, free, vmem, vmem),
            scratch_shapes=scratch,
            compiler_params=pltpu.CompilerParams(
                collective_id=0, has_side_effects=True, vmem_limit_bytes=60 * 2**20
            ),
        )(grad_out, chosen, counts, queries, keys, values, router_logit, out_weight)
        dq, dk, dv, dl, dw = pl.pallas_call(
            hand_out,
            out_shape=(grads, grads, grads) + results[2:],
            in_specs=[vmem] * 4,
            out_specs=(vmem,) * 5,
        )(*parts)
        return dq, dk, dv, dl, dw.T

    return jax.shard_map(
        on_device,
        mesh=mesh,
        in_specs=(
            P("dp", "ctx", None),
            P("dp", "ctx"),
            P("dp", "ctx"),
            P("dp", "ctx", None),
            P("dp", "ctx", None),
            P("dp", "ctx", None),
            P("dp", "ctx"),
            P(),
        ),
        out_specs=(
            P("dp", "ctx", None),
            P("dp", "ctx", None),
            P("dp", "ctx", None),
            P("dp", "ctx"),
            P(None, "ctx"),
        ),
        check_vma=False,
    )
```
